128 devices in a mesh: tm: 8 (over z, core), expert: 16 (over y, x).
Axes of the slice: x: 4, y: 4, z: 4, core: 2. Of those that a mesh axis runs over, the one named last changes fastest.
Arguments:
- frames: bfloat16 [16, 2048, 1024], P('expert', 'tm'), may hold values from -6 to 6
- routes: int32 [16, 2048, 2], P('expert', 'tm'), may hold values from 0 to 31, all different within a row; in each aligned block of 256 rows (0 to 255, 256 to 511, ..., all dimensions but the last counted through in order) at most 32 rows name the same one
- gates: float32 [16, 2048, 2], P('expert', 'tm'), may hold values from 0.2 to 1
- w_in: bfloat16 [32, 1024, 2048], P('expert', None, 'tm'), may hold values from -0.1875 to 0.1875
- w_out: bfloat16 [32, 2048, 1024], P('expert', 'tm'), may hold values from -0.125 to 0.125
- kernel: float32 [31, 1024], replicated, may hold values from -1 to 1
- gain: float32 [1024], replicated, may hold values from 0.1 to 1.9
- cotangent: bfloat16 [16, 2048, 1024], P('expert', 'tm'), may hold values from -6 to 6
Outputs:
- mixed: bfloat16 [16, 2048, 1024], P('expert', 'tm')
- input_grad: bfloat16 [16, 2048, 1024], P('expert', 'tm')
- w_in_grad: bfloat16 [32, 1024, 2048], P('expert', None, 'tm')
- w_out_grad: bfloat16 [32, 2048, 1024], P('expert', 'tm')
- kernel_grad: float32 [31, 1024], replicated
- gain_grad: float32 [1024], replicated
The draws below stay inside these ranges and needn't reach their ends.
Inputs may be any that keep to these rules, and one draw needn't show every extreme that they name: `routes`: the two ids of a frame differ; among the 256 frames of one block no id appears more than 32 times, and some id appears exactly 32 times in every block.
All inputs are finite; a program needn't handle non-finite values.
Results may differ from the reference program's by a relative error of at most 0.017.
Values may be sent and summed in bfloat16 or wider, within the bound.
No kernel may reach another device: no remote copies, remote signals or barrier semaphores. Data moves between devices by JAX's collectives and lax.ppermute only.
A program may use at most 128 MiB of HBM per device.

```python
import math
import jax
import jax.numpy as jnp
import numpy as np
from jax import lax

D = 1024
FF = 2048
KW = 31
TOK_DEV = 256
EXPERTS = 32
CAP = 32
UTTS = 16
FRAMES = 2048
N_TM = 8


def level_of(stream_key, dims, pieces, low, high):
    level, own = 1.0, jax.random.fold_in(stream_key, 6)
    for dim, parts in pieces:
        steps = jnp.exp(jax.random.uniform(jax.random.fold_in(own, dim), (parts,), jnp.float32, low / len(pieces), high / len(pieces)))
        level = level * jnp.repeat(steps, dims[dim] // parts).reshape([-1 if axis == dim else 1 for axis in range(len(dims))])
    return level


def shared_out(own_key, own, number, rows, amount, top, bound, lean):
    sequence = jax.random.permutation(own_key, amount)
    packed, ordinary = portions_of(amount, rows * top, bound, lean, True), portions_of(amount, rows * top, bound, lean, False)
    places = jnp.arange(amount)

    def named(sizes, rotation):
        used = int((sizes > 0).sum())
        fixed = max(1, used // 4)
        shifted = fixed + (places - fixed + rotation * (used - fixed)) % max(1, amount - fixed)
        return jnp.zeros((amount,), jnp.int32).at[sequence[jnp.where(places < fixed, places, shifted)]].set(jnp.asarray(sizes, jnp.int32))

    sizes = jnp.where(number % 4 == 0, named(packed, number // 4), named(ordinary, number - number // 4 - 1))
    mixed = jax.random.permutation(jax.random.fold_in(own, 3), amount)
    giver, receiver = mixed[0:amount // 2 * 2:2], mixed[1:amount // 2 * 2:2]
    slack = jnp.minimum(sizes[giver] - 1, bound - sizes[receiver]) // 2
    slack = jnp.where((giver == sequence[0]) | (receiver == sequence[0]) | (sizes[receiver] == 0), 0, jnp.maximum(slack, 0))
    shifted = jax.random.randint(jax.random.fold_in(own, 4), (amount // 2,), 0, 1 << 20) % (slack + 1)
    sizes = sizes.at[giver].add(-shifted).at[receiver].add(shifted)
    labels = jnp.searchsorted(jnp.cumsum(sizes), jnp.arange(rows * top), side="right").astype(jnp.int32)
    listing = labels.reshape(top, rows).T
    listing = listing[jax.random.permutation(jax.random.fold_in(own, 1), rows)]
    rotation = jax.random.randint(jax.random.fold_in(own, 2), (rows, 1), 0, top)
    return jnp.take_along_axis(listing, (jnp.arange(top)[None, :] + rotation) % top, axis=1)


def portions_of(amount, total, bound, skew, full):
    loads = [(1 << 20) // math.isqrt(standing ** skew) + 1 for standing in range(1, amount + 1)]
    largest = bound if full else min(bound, max(-(-total // amount), total * loads[0] // sum(loads)))
    least = 1 if total - largest >= amount - 1 else 0
    holding, rest = [largest] + [least] * (amount - 1), total - largest - least * (amount - 1)
    while rest > 0:
        movable = [i for i in range(1, amount) if holding[i] < largest] or [i for i in range(1, amount) if holding[i] < bound]
        mass, left = sum([loads[i] for i in movable]), rest
        for i in movable:
            addition = min(bound - holding[i], max(1, left * loads[i] // mass), rest)
            holding[i] = holding[i] + addition
            rest = rest - addition
    return np.array(holding)


def bell_draw(stream_key, extent, deviation, bound, cuts=(), kind=jnp.bfloat16):
    factor_of = level_of(stream_key, extent, cuts, -0.22, 0.18) if cuts else 1.0
    array = jax.random.normal(stream_key, extent, jnp.float32) * deviation * factor_of
    return jnp.minimum(jnp.maximum(array, -bound), bound).astype(kind)


def setup_inputs(seed: int = 0) -> dict:
    key_list = jax.random.split(jax.random.key(seed), 9)
    frames = bell_draw(key_list[0], (UTTS, FRAMES, D), 1.0, 6.0, ((0, 16), (1, 8)))
    routes_keys = jax.random.split(jax.random.fold_in(key_list[1], 1), UTTS * FRAMES // TOK_DEV)
    routes_turns = jax.random.permutation(jax.random.fold_in(key_list[1], 3), UTTS * FRAMES // TOK_DEV)
    routes = jax.vmap(lambda own, number: shared_out(jax.random.fold_in(key_list[1], 2), own, number, TOK_DEV, EXPERTS, 2, CAP, 2))(routes_keys, routes_turns).reshape((UTTS, FRAMES, 2))
    gates = jnp.clip(0.2 + 0.8 * jax.random.uniform(key_list[2], (UTTS, FRAMES, 2), jnp.float32) ** level_of(key_list[2], (UTTS, FRAMES, 2), ((0, 16), (1, 8)), -0.2, 0.2), 0.2, 1.0)
    w_in = bell_draw(key_list[3], (EXPERTS, D, FF), D ** -0.5, 0.1875, ((0, 16), (2, 8)))
    w_out = bell_draw(key_list[4], (EXPERTS, FF, D), FF ** -0.5, 0.125, ((0, 16), (1, 8)))
    kernel = bell_draw(key_list[5], (KW, D), KW ** -0.5, 1.0, (), jnp.float32)
    gain = jnp.clip(1.0 + 0.18 * jax.random.normal(key_list[6], (D,), jnp.float32), 0.1, 1.9)
    cotangent = bell_draw(key_list[7], (UTTS, FRAMES, D), 1.0, 6.0, ((0, 16), (1, 8)))
    return {"frames": frames, "routes": routes, "gates": gates, "w_in": w_in, "w_out": w_out, "kernel": kernel, "gain": gain, "cotangent": cotangent}


def slot_index(route_rows, experts, capacity):
    flat_ids = route_rows.reshape(-1).astype(jnp.int32)
    one_hot = (flat_ids[:, None] == jnp.arange(experts, dtype=jnp.int32)[None, :]).astype(jnp.int32)
    earlier = jnp.cumsum(one_hot, axis=0) - one_hot
    return (flat_ids * capacity + lax.optimization_barrier(jnp.sum(one_hot * earlier, axis=1))).astype(jnp.int32)

def silu_slope(pre_act):
    sigmoid_val = jax.nn.sigmoid(pre_act)
    return sigmoid_val * (1.0 + pre_act * (1.0 - sigmoid_val))

def place_rows(slots, values):
    return jnp.zeros((EXPERTS * CAP, D), jnp.bfloat16).at[slots].set(values)

def reference(frames, routes, gates, w_in, w_out, kernel, gain, cotangent):
    reach = (KW - 1) // 2
    padded = jnp.pad(frames, ((0, 0), (reach, reach), (0, 0)))
    hidden = frames.astype(jnp.float32)
    for offset in range(KW):
        hidden = hidden + kernel[offset] * padded[:, offset:offset + FRAMES].astype(jnp.float32)
    inv_rms = lax.rsqrt(lax.optimization_barrier(jnp.mean(hidden * hidden, axis=-1, keepdims=True)) + 1e-06)
    normed = (hidden * inv_rms * gain).astype(jnp.bfloat16)
    w_in_wide = w_in.astype(jnp.float32)
    w_out_wide = w_out.astype(jnp.float32)

    def one_block(carry, block_index):
        start = (block_index * TOK_DEV).astype(jnp.int32)
        rows = lax.dynamic_slice_in_dim(normed, start, TOK_DEV, 1)
        route_blk = lax.dynamic_slice_in_dim(routes, start, TOK_DEV, 1)
        gate_blk = lax.dynamic_slice_in_dim(gates, start, TOK_DEV, 1)
        grad_blk = lax.dynamic_slice_in_dim(cotangent, start, TOK_DEV, 1).astype(jnp.float32)
        slots = jax.vmap(lambda one: slot_index(one, EXPERTS, CAP))(route_blk)
        repeated = jnp.repeat(rows, 2, axis=1)
        buffer = jax.vmap(place_rows)(slots, repeated).reshape(UTTS, EXPERTS, CAP, D)
        pre_act = jnp.einsum('uecd,edf->uecf', buffer.astype(jnp.float32), w_in_wide)
        activated = jax.nn.silu(pre_act).astype(jnp.bfloat16)
        expert_out = jnp.einsum('uecf,efd->uecd', activated.astype(jnp.float32), w_out_wide).astype(jnp.bfloat16)
        picked = jnp.take_along_axis(expert_out.reshape(UTTS, EXPERTS * CAP, D), slots[:, :, None], axis=1)
        picked = picked.astype(jnp.float32).reshape(UTTS, TOK_DEV, 2, D)
        combined = lax.optimization_barrier(jnp.sum(gate_blk[..., None] * picked, axis=2))
        slot_grads = (gate_blk[..., None] * grad_blk[:, :, None, :]).astype(jnp.bfloat16).reshape(UTTS, 2 * TOK_DEV, D)
        grad_buffer = jax.vmap(place_rows)(slots, slot_grads).reshape(UTTS, EXPERTS, CAP, D)
        act_grad = jnp.einsum('uecd,efd->uecf', grad_buffer.astype(jnp.float32), w_out_wide)
        pre_grad = (act_grad * silu_slope(pre_act)).astype(jnp.bfloat16)
        part_out = jnp.einsum('uecf,uecd->efd', activated.astype(jnp.float32), grad_buffer.astype(jnp.float32)).astype(jnp.bfloat16)
        part_in = jnp.einsum('uecd,uecf->edf', buffer.astype(jnp.float32), pre_grad.astype(jnp.float32)).astype(jnp.bfloat16)
        row_grads = jnp.einsum('uecf,edf->uecd', pre_grad.astype(jnp.float32), w_in_wide).astype(jnp.bfloat16)
        back = jnp.take_along_axis(row_grads.reshape(UTTS, EXPERTS * CAP, D), slots[:, :, None], axis=1)
        norm_grad = lax.optimization_barrier(jnp.sum(back.astype(jnp.float32).reshape(UTTS, TOK_DEV, 2, D), axis=2))
        carry = (carry[0] + part_in.astype(jnp.float32), carry[1] + part_out.astype(jnp.float32))
        return (carry, (combined, norm_grad))
    init = (jnp.zeros((EXPERTS, D, FF), jnp.float32), jnp.zeros((EXPERTS, FF, D), jnp.float32))
    sums, outs = lax.scan(one_block, init, jnp.arange(N_TM, dtype=jnp.int32))
    combined = jnp.transpose(outs[0], (1, 0, 2, 3)).reshape(UTTS, FRAMES, D)
    norm_grad = jnp.transpose(outs[1], (1, 0, 2, 3)).reshape(UTTS, FRAMES, D)
    mixed = (hidden + combined).astype(jnp.bfloat16)
    out_grad = cotangent.astype(jnp.float32)
    scaled_grad = norm_grad * gain
    hidden_grad = out_grad + inv_rms * scaled_grad - hidden * inv_rms ** 3 * lax.optimization_barrier(jnp.mean(scaled_grad * hidden, axis=-1, keepdims=True))
    gain_grad = lax.optimization_barrier(jnp.sum(norm_grad * hidden * inv_rms, axis=(0, 1)))
    grad_pad = jnp.pad(hidden_grad, ((0, 0), (reach, reach), (0, 0)))
    input_grad = hidden_grad
    taps = []
    for offset in range(KW):
        input_grad = input_grad + kernel[offset] * grad_pad[:, 2 * reach - offset:2 * reach - offset + FRAMES]
        taps.append(lax.optimization_barrier(jnp.sum(hidden_grad * padded[:, offset:offset + FRAMES].astype(jnp.float32), axis=(0, 1))))
    kernel_grad = jnp.stack(taps)
    return (mixed, input_grad.astype(jnp.bfloat16), sums[0].astype(jnp.bfloat16), sums[1].astype(jnp.bfloat16), kernel_grad, gain_grad)
```

```python
import jax
import jax.numpy as jnp
from jax import lax
from jax.sharding import PartitionSpec as P

BF = jnp.bfloat16
F32 = jnp.float32


def ring(count, step):
    return [(i, (i + step) % count) for i in range(count)]


def line(count, step):
    return [(i, i + step) for i in range(count) if 0 <= i + step < count]


def xor(count, step):
    return [(i, i ^ step) for i in range(count)]


def slot_index(route_rows, experts, capacity):
    ids = route_rows[:, :, None] == jnp.arange(experts, dtype=jnp.int32)[None, None, :]
    both = jnp.sum(ids.astype(BF), axis=1)
    count = route_rows.shape[0]
    before = (jnp.arange(count)[:, None] > jnp.arange(count)[None, :]).astype(BF)
    earlier = jnp.dot(before, both, preferred_element_type=F32)
    rank = jnp.sum(jnp.where(ids, earlier[:, None, :], 0.0), axis=2).astype(jnp.int32)
    return route_rows * capacity + rank


def gather_ring(block, minus, plus):
    low = lax.ppermute(block, "tm", plus)
    high = lax.ppermute(block, "tm", minus)
    far = (lax.ppermute(low[:1], "tm", plus), lax.ppermute(high[1:], "tm", minus))
    return low, high, jnp.concatenate(far, axis=0)


def scatter_ring(own, low, high, far, minus, plus):
    far_up = lax.ppermute(far[:1], "tm", plus)
    far_down = lax.ppermute(far[1:], "tm", minus)
    up = jnp.concatenate([(high[:1].astype(F32) + far_up.astype(F32)).astype(BF), high[1:]], axis=0)
    down = jnp.concatenate([low[:1], (low[1:].astype(F32) + far_down.astype(F32)).astype(BF)], axis=0)
    from_low = lax.ppermute(up, "tm", plus)
    from_high = lax.ppermute(down, "tm", minus)
    return (own.astype(F32) + from_low.astype(F32) + from_high.astype(F32)).astype(BF)


def butterfly(part):
    for step in (1, 2, 4):
        part = part + lax.ppermute(part, "tm", xor(8, step))
    for step in (1, 2, 4, 8):
        part = part + lax.ppermute(part, "expert", xor(16, step))
    return part


def body(frames, routes, gates, w_in, w_out, kernel, gain, cotangent):
    tms = lax.axis_size("tm")
    owners = lax.axis_size("expert")
    count, width = frames.shape[1], frames.shape[2]
    local = w_in.shape[0]
    experts = local * owners
    capacity = 4 * count // experts
    taps = kernel.shape[0]
    reach = (taps - 1) // 2
    plus, minus, swap = ring(tms, 2), ring(tms, -2), xor(tms, 1)
    block = frames[0]
    low = lax.ppermute(block[count - reach :], "tm", line(tms, 1))
    high = lax.ppermute(block[:reach], "tm", line(tms, -1))
    wo = (w_out,) + gather_ring(w_out, minus, plus)
    wi = (w_in,) + gather_ring(w_in, minus, plus)

    slots = slot_index(routes[0], experts, capacity)
    places = jnp.arange(experts * capacity, dtype=jnp.int32)
    pick = [(slots[:, j, None] == places[None, :]).astype(BF) for j in range(2)]
    cot = cotangent[0].astype(F32)
    gate = gates[0]
    weighted = [(gate[:, j, None] * cot).astype(BF) for j in range(2)]
    gbuf = jnp.einsum("ks,kd->sd", jnp.concatenate(pick), jnp.concatenate(weighted), preferred_element_type=F32)

    def exchange(rows):
        return lax.all_to_all(
            rows.astype(BF).reshape(owners, local * capacity, width), "expert", split_axis=0, concat_axis=0, tiled=True
        )

    def both_cores(rows):
        other = lax.ppermute(rows, "tm", swap)
        return jnp.stack([rows, other]).reshape(2, owners, local, capacity, width)

    grad_rows = both_cores(exchange(gbuf))
    padded = jnp.concatenate([low, block, high])
    hidden = block.astype(F32)
    for offset in range(taps):
        hidden = hidden + kernel[offset] * padded[offset : offset + count].astype(F32)
    inv_rms = lax.rsqrt(jnp.mean(hidden * hidden, axis=-1, keepdims=True) + 1e-06)
    normed = (hidden * inv_rms * gain).astype(BF)
    buf = jnp.einsum("ks,kd->sd", pick[0] + pick[1], normed, preferred_element_type=F32)
    rows = both_cores(exchange(buf))

    acts, pre_grads, pins, pouts = [], [], [], []
    for part in range(4):
        pre = jnp.einsum("nsecd,edf->nsecf", rows, wi[part], preferred_element_type=F32)
        sig = jax.nn.sigmoid(pre)
        act = (pre * sig).astype(BF)
        act_grad = jnp.einsum("nsecd,efd->nsecf", grad_rows, wo[part], preferred_element_type=F32)
        pre_grad = (act_grad * (sig * (1.0 + pre * (1.0 - sig)))).astype(BF)
        acts.append(act)
        pre_grads.append(pre_grad)
        pins.append(jnp.einsum("nsecd,nsecf->edf", rows, pre_grad, preferred_element_type=F32).astype(BF))
        pouts.append(jnp.einsum("nsecf,nsecd->efd", act, grad_rows, preferred_element_type=F32).astype(BF))
    wi_all = jnp.concatenate(wi, axis=2)
    wo_all = jnp.concatenate(wo, axis=1)
    row_grads = jnp.einsum(
        "nsecf,edf->nsecd", jnp.concatenate(pre_grads, axis=-1), wi_all, preferred_element_type=F32
    )
    outs = jnp.einsum("nsecf,efd->nsecd", jnp.concatenate(acts, axis=-1), wo_all, preferred_element_type=F32)

    def back(both):
        other = lax.ppermute(both[1].astype(BF), "tm", swap)
        return exchange(both[0] + other.astype(F32)).reshape(experts * capacity, width)

    returned_grads = back(row_grads)
    out_sum = scatter_ring(pouts[0], pouts[1], pouts[2], pouts[3], minus, plus)
    in_sum = scatter_ring(pins[0], pins[1], pins[2], pins[3], minus, plus)
    norm_grad = jnp.dot(pick[0] + pick[1], returned_grads, preferred_element_type=F32)
    scaled_grad = norm_grad * gain
    hidden_grad = (
        cot + inv_rms * scaled_grad - hidden * inv_rms**3 * jnp.mean(scaled_grad * hidden, axis=-1, keepdims=True)
    )
    gain_part = jnp.sum(norm_grad * hidden * inv_rms, axis=0)
    rounded = hidden_grad.astype(BF)
    grad_low = lax.ppermute(rounded[count - reach :], "tm", line(tms, 1))
    grad_high = lax.ppermute(rounded[:reach], "tm", line(tms, -1))
    parts = [jnp.sum(hidden_grad * padded[k : k + count].astype(F32), axis=0) for k in range(taps)]
    summed = butterfly(jnp.stack(parts + [gain_part]))
    grad_pad = jnp.concatenate([grad_low, rounded, grad_high])
    input_grad = hidden_grad
    for k in range(taps):
        input_grad = input_grad + kernel[k] * grad_pad[2 * reach - k : 2 * reach - k + count].astype(F32)
    returned = back(outs)
    picked = [jnp.dot(pick[j], returned, preferred_element_type=F32) for j in range(2)]
    mixed = hidden + gate[:, 0:1] * picked[0] + gate[:, 1:2] * picked[1]
    return (
        mixed.astype(BF)[None],
        input_grad.astype(BF)[None],
        in_sum,
        out_sum,
        summed[:taps],
        summed[taps],
    )


def solution(mesh):
    return jax.shard_map(
        body,
        mesh=mesh,
        in_specs=(
            P("expert", "tm", None),
            P("expert", "tm", None),
            P("expert", "tm", None),
            P("expert", None, "tm"),
            P("expert", "tm", None),
            P(),
            P(),
            P("expert", "tm", None),
        ),
        out_specs=(
            P("expert", "tm", None),
            P("expert", "tm", None),
            P("expert", None, "tm"),
            P("expert", "tm", None),
            P(),
            P(),
        ),
        check_vma=False,
    )
```

```python
import functools

import jax
import jax.numpy as jnp
from jax import lax
from jax.experimental import pallas as pl
from jax.experimental.pallas import tpu as pltpu
from jax.sharding import PartitionSpec as P

BF = jnp.bfloat16
F32 = jnp.float32
EDGE = 16
PARAMS = pltpu.CompilerParams(vmem_limit_bytes=56 * 1024 * 1024)


def ring(count, step):
    return [(i, (i + step) % count) for i in range(count)]


def line(count, step):
    return [(i, i + step) for i in range(count) if 0 <= i + step < count]


def xor(count, step):
    return [(i, i ^ step) for i in range(count)]


def shape(dims, dtype):
    return jax.ShapeDtypeStruct(dims, dtype)


def mm(left, right, dim_left=1, dim_right=0):
    return lax.dot_general(left, right, (((dim_left,), (dim_right,)), ((), ())), preferred_element_type=F32)


def cotangent_slots(experts, capacity, ids_ref, gates_ref, cot_ref, gbuf_ref, rows_ref, cols_ref):
    count = ids_ref.shape[1]
    expert = lax.broadcasted_iota(jnp.int32, (experts, count), 0)
    hot = [(expert == ids_ref[j : j + 1, :]).astype(F32) for j in range(2)]
    frame = lax.broadcasted_iota(jnp.int32, (count, count), 0)
    later = lax.broadcasted_iota(jnp.int32, (count, count), 1)
    earlier = mm((hot[0] + hot[1]).astype(BF), (frame < later).astype(BF))
    rows = [
        ids_ref[j : j + 1, :].astype(F32) * capacity + jnp.sum(hot[j] * earlier, axis=0, keepdims=True)
        for j in range(2)
    ]
    table = jnp.concatenate([gates_ref[...], rows[0], rows[1], jnp.zeros((124, count), F32)], axis=0)
    cols = table.T
    cols_ref[...] = cols
    rows_ref[...] = table[:8]
    place = lax.broadcasted_iota(jnp.int32, (experts * capacity, count), 0)
    spread = [(place == rows[j].astype(jnp.int32)).astype(F32).astype(BF) for j in range(2)]
    cot = cot_ref[...].astype(F32)
    weighted = [(cols[:, j : j + 1] * cot).astype(BF) for j in range(2)]
    gbuf_ref[...] = mm(jnp.concatenate(spread, axis=1), jnp.concatenate(weighted, axis=0)).astype(BF)


def fill(pad, low_ref, mid, high_ref):
    count = mid.shape[0]
    pad[0:EDGE, :] = low_ref[...].astype(F32)
    pad[EDGE : EDGE + count, :] = mid
    pad[EDGE + count : 2 * EDGE + count, :] = high_ref[...].astype(F32)


def convolve(pad, taps_ref, store, count, taps, flip):
    width = pad.shape[1]
    step = 64
    for lane in range(0, width, 128):
        lanes = slice(lane, lane + 128)
        for row in range(0, count, step):
            total = pad[EDGE + row : EDGE + row + step, lanes]
            for k in range(taps):
                at = row + (taps - k if flip else k + 1)
                total = total + taps_ref[k : k + 1, lanes] * pad[at : at + step, lanes]
            store(row, lanes, total)


def norm_slots(capacity_all, frames_ref, low_ref, high_ref, taps_ref, gain_ref, rows_ref, buf_ref, hidden_ref, pad):
    count = frames_ref.shape[0]
    taps = taps_ref.shape[0]
    fill(pad, low_ref, frames_ref[...].astype(F32), high_ref)

    def store(row, lanes, total):
        hidden_ref[row : row + 64, lanes] = total

    convolve(pad, taps_ref, store, count, taps, False)
    hidden = hidden_ref[...]
    inv = lax.rsqrt(jnp.mean(hidden * hidden, axis=-1, keepdims=True) + 1e-06)
    normed = (hidden * inv * gain_ref[...]).astype(BF)
    place = lax.broadcasted_iota(jnp.int32, (capacity_all, count), 0)
    slots = rows_ref[...].astype(jnp.int32)
    spread = ((place == slots[2:3, :]) | (place == slots[3:4, :])).astype(F32).astype(BF)
    buf_ref[...] = mm(spread, normed).astype(BF)


def picks(cols, capacity_all):
    count = cols.shape[0]
    place = lax.broadcasted_iota(jnp.int32, (count, capacity_all), 1)
    slots = cols.astype(jnp.int32)
    return [place == slots[:, 2 + j : 3 + j] for j in range(2)]


def hidden_grads(
    back_ref, cols_ref, hidden_ref, gain_ref, cot_ref, frames_ref, low_ref, high_ref, taps_ref,
    grad_ref, first_ref, last_ref, part_ref, pad,
):
    count = frames_ref.shape[0]
    taps = taps_ref.shape[0]
    width = frames_ref.shape[1]
    fill(pad, low_ref, frames_ref[...].astype(F32), high_ref)
    pick = picks(cols_ref[...], back_ref.shape[0])
    norm_grad = mm((pick[0] | pick[1]).astype(F32).astype(BF), back_ref[...])
    hidden = hidden_ref[...]
    inv = lax.rsqrt(jnp.mean(hidden * hidden, axis=-1, keepdims=True) + 1e-06)
    scaled = norm_grad * gain_ref[...]
    mean = jnp.mean(scaled * hidden, axis=-1, keepdims=True)
    grad_ref[...] = cot_ref[...].astype(F32) + inv * scaled - hidden * (inv * inv * inv * mean)
    first_ref[...] = grad_ref[0:EDGE, :].astype(BF)
    last_ref[...] = grad_ref[count - EDGE : count, :].astype(BF)
    part_ref[taps : taps + 1, :] = jnp.sum(norm_grad * hidden * inv, axis=0, keepdims=True)
    for lane in range(0, width, 128):
        lanes = slice(lane, lane + 128)
        for k in range(taps):
            product = grad_ref[:, lanes] * pad[k + 1 : k + 1 + count, lanes]
            part_ref[k : k + 1, lanes] = jnp.sum(product, axis=0, keepdims=True)


def input_grads(grad_ref, low_ref, high_ref, taps_ref, out_ref, pad):
    count = grad_ref.shape[0]
    fill(pad, low_ref, grad_ref[...], high_ref)

    def store(row, lanes, total):
        out_ref[row : row + 64, lanes] = total.astype(BF)

    convolve(pad, taps_ref, store, count, taps_ref.shape[0], True)


def mix(back_ref, cols_ref, hidden_ref, out_ref):
    cols = cols_ref[...]
    total = hidden_ref[...]
    for j, pick in enumerate(picks(cols, back_ref.shape[0])):
        total = total + cols[:, j : j + 1] * mm(pick.astype(F32).astype(BF), back_ref[...])
    out_ref[...] = total.astype(BF)


def both_rows(own_ref, other_ref):
    width = own_ref.shape[-1]
    return jnp.concatenate([own_ref[...].reshape(-1, width), other_ref[...].reshape(-1, width)], axis=0)


def store_rows(value, own_ref, other_ref):
    half = value.shape[0] // 2
    own_ref[...] = value[:half].astype(BF).reshape(own_ref.shape)
    other_ref[...] = value[half:].astype(BF).reshape(other_ref.shape)


def pack(in_ref, out_ref, packed_ref):
    held, width = out_ref.shape[1:]
    for q in range(width // held):
        rows = slice(q * held, q * held + held)
        packed_ref[0, 0, :, rows] = in_ref[0, rows, :]
    packed_ref[0, 1] = out_ref[0]


def part_in(packed):
    held, width = packed.shape
    return jnp.concatenate([packed[:, q * held : (q + 1) * held] for q in range(width // held)], axis=0)


def far_of(far0, far1, which):
    return jnp.where(pl.program_id(0) == 0, far0[0, which], far1[0, which])


def act_grads(g0, g1, w0, w1, w2, ga_ref):
    grads = both_rows(g0, g1)
    held = w0.shape[2]
    for part, w in enumerate((w0, w1, w2)):
        ga_ref[0, :, part * held : (part + 1) * held] = mm(grads, w[0, 0], 1, 1).astype(BF)


def keep(refs, value):
    for e, ref in enumerate(refs):

        @pl.when(pl.program_id(0) == e)
        def _(ref=ref):
            for which in range(2):
                ref[0, which] = value[which]


def experts_main(
    x0, x1, g0, g1, ga_ref, w0, w1, w2, far0, far1, act_ref, pg_ref, own_ref, other_ref, grad0, grad1
):
    rows, grads = both_rows(x0, x1), both_rows(g0, g1)
    held = w0.shape[2]
    parts = [part_in(w[0, 0]) for w in (w0, w1, w2)] + [part_in(far_of(far0, far1, 0))]
    for part in (3, 0, 1, 2):
        columns = slice(part * held, part * held + held)
        pre = mm(rows, parts[part])
        if part == 3:
            act_grad = mm(grads, far_of(far0, far1, 1), 1, 1)
        else:
            act_grad = ga_ref[0, :, columns].astype(F32)
        sig = 0.5 * jnp.tanh(0.5 * pre) + 0.5
        act = (pre * sig).astype(BF)
        pre_grad = (act_grad * (sig * (1.0 + pre * (1.0 - sig)))).astype(BF)
        act_ref[0, :, columns] = act
        pg_ref[0, :, columns] = pre_grad
        if part == 3:
            keep((grad0, grad1), (mm(pre_grad, rows, 0, 0).astype(BF), mm(act, grads, 0, 0).astype(BF)))
    store_rows(mm(pg_ref[0], jnp.concatenate(parts, axis=1), 1, 1), own_ref, other_ref)


def experts_out(act, w0, w1, w2, far0, far1, own_ref, other_ref):
    parts = [w[0, 0] for w in (w0, w1, w2)] + [far_of(far0, far1, 0)]
    store_rows(mm(act[0], jnp.concatenate(parts, axis=0)), own_ref, other_ref)


def own_grads(x0, x1, g0, g1, act, pg, in_ref, out_ref):
    in_ref[0] = mm(pg[0], both_rows(x0, x1), 0, 0).astype(BF)
    out_ref[0] = mm(act[0], both_rows(g0, g1), 0, 0).astype(BF)


def sent_grads(x0, x1, g0, g1, act1, act2, pg1, pg2, far_up, far_down, up_in, up_out, down_in, down_out):
    expert = pl.program_id(0)
    rows, grads = both_rows(x0, x1), both_rows(g0, g1)
    for act, pg, far, mine, in_ref, out_ref in (
        (act1, pg1, far_down, 1, down_in, down_out),
        (act2, pg2, far_up, 0, up_in, up_out),
    ):
        in_grad, out_grad = mm(pg[0], rows, 0, 0), mm(act[0], grads, 0, 0)
        held = expert == mine
        in_ref[0] = (in_grad + jnp.where(held, far[0, 0].astype(F32), 0.0)).astype(BF)
        out_ref[0] = (out_grad + jnp.where(held, far[0, 1].astype(F32), 0.0)).astype(BF)


def final_in(own, up, down, out_ref):
    total = own[0].astype(F32) + up[0].astype(F32) + down[0].astype(F32)
    out_ref[0] = total.T.astype(BF)


def final_out(own, up, down, out_ref):
    out_ref[0] = (own[0].astype(F32) + up[0].astype(F32) + down[0].astype(F32)).astype(BF)


def cost(micros):
    return pl.CostEstimate(flops=micros * 1_000_000_000, transcendentals=0, bytes_accessed=micros * 1_000_000)


def call(kernel, outs, micros, scratch=()):
    return pl.pallas_call(
        kernel, out_shape=outs, scratch_shapes=list(scratch), compiler_params=PARAMS, cost_estimate=cost(micros)
    )


def after(value, *others):
    return lax.optimization_barrier((value,) + others)[0]


def sum_all(part):
    for axis, count, steps in (
        ("expert", 16, (1, 2, 3)),
        ("expert", 16, (4, 8, 12)),
        ("tm", 8, (1,)),
        ("tm", 8, (2, 4, 6)),
    ):
        sent = part.astype(BF)
        for step in steps:
            part = part + lax.ppermute(sent, axis, xor(count, step)).astype(F32)
    return part


def body(frames, routes, gates, w_in, w_out, kernel, gain, cotangent):
    tms = lax.axis_size("tm")
    owners = lax.axis_size("expert")
    count, width = frames.shape[1], frames.shape[2]
    local, held = w_in.shape[0], w_in.shape[2]
    experts = local * owners
    capacity = 4 * count // experts
    slots = experts * capacity
    taps = kernel.shape[0]
    plus, minus, swap = ring(tms, 2), ring(tms, -2), xor(tms, 1)
    block, cot, gain_row = frames[0], cotangent[0], gain[None]
    both = 2 * owners * capacity
    token_shape = shape((owners, local, capacity, width), BF)
    wide_shape = shape((local, both, 4 * held), BF)
    unit_shape = shape((local, held, width), BF)
    one_shape = shape((1, 2, held, width), BF)
    token_spec = pl.BlockSpec((owners, 1, capacity, width), lambda e: (0, e, 0, 0))
    in_spec = pl.BlockSpec((1, width, held), lambda e: (e, 0, 0))
    out_spec = pl.BlockSpec((1, held, width), lambda e: (e, 0, 0))
    packed_spec = pl.BlockSpec((1, 2, held, width), lambda e: (e, 0, 0, 0))
    one_spec = pl.BlockSpec((1, 2, held, width), lambda e: (0, 0, 0, 0))
    wide_spec = pl.BlockSpec((1, both, 4 * held), lambda e: (e, 0, 0))
    most_spec = pl.BlockSpec((1, both, 3 * held), lambda e: (e, 0, 0))

    def part_spec(part):
        return pl.BlockSpec((1, both, held), lambda e: (e, 0, part))

    def per_expert(kernel, micros, in_specs, out_specs, out_shape):
        return pl.pallas_call(
            kernel,
            grid=(local,),
            in_specs=in_specs,
            out_specs=out_specs,
            out_shape=out_shape,
            compiler_params=PARAMS,
            cost_estimate=cost(micros),
        )

    def exchange(rows):
        return lax.all_to_all(
            rows.reshape(owners, local * capacity, width), "expert", split_axis=0, concat_axis=0, tiled=True
        )

    def tokens(value):
        return value.reshape(owners, local, capacity, width)

    low = lax.ppermute(block[count - EDGE :], "tm", line(tms, 1))
    high = lax.ppermute(block[:EDGE], "tm", line(tms, -1))
    packed = per_expert(pack, 3, [in_spec, out_spec], packed_spec, shape((local, 2, held, width), BF))(w_in, w_out)
    packed = after(packed, low, high)
    w_low = lax.ppermute(packed, "tm", plus)
    w_high = lax.ppermute(packed, "tm", minus)

    gbuf, slot_rows, slot_cols = call(
        functools.partial(cotangent_slots, experts, capacity),
        (shape((slots, width), BF), shape((8, count), F32), shape((count, 128), F32)),
        4,
    )(routes[0].T, gates[0].T, cot)
    g_own = exchange(gbuf)
    pad = pltpu.VMEM((count + 2 * EDGE, width), F32)
    buf, hidden = call(
        functools.partial(norm_slots, slots), (shape((slots, width), BF), shape((count, width), F32)), 9, [pad]
    )(block, low, high, kernel, gain_row, slot_rows)
    x_own = exchange(after(buf, g_own))
    g_own = tokens(after(g_own, buf))
    g_other = lax.ppermute(g_own, "tm", swap)
    far0 = lax.ppermute(w_low[:1], "tm", plus)
    far1 = lax.ppermute(w_high[1:], "tm", minus)
    weights = (packed, w_low, w_high, far0, far1)
    weight_specs = [packed_spec] * 3 + [one_spec] * 2
    other_half = pl.BlockSpec((1, 1, held, width), lambda e: (e, 1, 0, 0))
    act_grad = per_expert(
        act_grads, 7, [token_spec] * 2 + [other_half] * 3, most_spec, shape((local, both, 3 * held), BF)
    )(g_own, g_other, packed, w_low, w_high)
    x_own = tokens(after(x_own, act_grad, far0, far1))
    x_other = lax.ppermute(x_own, "tm", swap)
    rows = (x_own, x_other, g_own, g_other)

    half_spec = pl.BlockSpec((1, 1, held, width), lambda e: (e, 0, 0, 0))
    act, pre_grad, r_own, r_other, far_grad0, far_grad1 = per_expert(
        experts_main,
        22,
        [token_spec] * 4 + [most_spec] + [half_spec] * 3 + [one_spec] * 2,
        (wide_spec, wide_spec, token_spec, token_spec, one_spec, one_spec),
        (wide_shape, wide_shape, token_shape, token_shape, one_shape, one_shape),
    )(*rows, act_grad, *weights)
    far_up = lax.ppermute(far_grad0, "tm", plus)
    far_down = lax.ppermute(far_grad1, "tm", minus)

    def summed_cores(own, other):
        swapped = lax.ppermute(other, "tm", swap)
        return (own.astype(F32) + swapped.astype(F32)).astype(BF)

    def back(total):
        return exchange(total).reshape(slots, width)

    far_half = pl.BlockSpec((1, 1, held, width), lambda e: (0, 1, 0, 0))
    back_grads = back(summed_cores(r_own, r_other))
    own_in, own_out = per_expert(
        own_grads, 6, [token_spec] * 4 + [part_spec(0)] * 2, (out_spec, out_spec), (unit_shape, unit_shape)
    )(*rows, act, pre_grad)
    o_own, o_other = per_expert(
        experts_out, 10, [wide_spec] + [other_half] * 3 + [far_half] * 2, (token_spec, token_spec), (token_shape, token_shape)
    )(act, *weights)
    up_in, up_out, down_in, down_out = per_expert(
        sent_grads,
        9,
        [token_spec] * 4 + [part_spec(1), part_spec(2)] * 2 + [one_spec] * 2,
        (out_spec,) * 4,
        (unit_shape,) * 4,
    )(*rows, act, act, pre_grad, pre_grad, far_up, far_down)
    o_sum = summed_cores(o_own, o_other)
    back_grads = after(back_grads, up_in, up_out, down_in, down_out, own_in, own_out, o_sum)
    up_in = lax.ppermute(up_in, "tm", plus)
    down_in = lax.ppermute(down_in, "tm", minus)

    hidden_grad, first, last, part = call(
        hidden_grads,
        (
            shape((count, width), F32),
            shape((EDGE, width), BF),
            shape((EDGE, width), BF),
            shape((taps + 1, width), F32),
        ),
        10,
        [pad],
    )(back_grads, slot_cols, hidden, gain_row, cot, block, low, high, kernel)
    grad_low = lax.ppermute(last, "tm", line(tms, 1))
    grad_high = lax.ppermute(first, "tm", line(tms, -1))
    up_out = lax.ppermute(after(up_out, grad_low), "tm", plus)
    down_out = lax.ppermute(after(down_out, grad_high), "tm", minus)
    back_outs = back(after(o_sum, back_grads))
    summed = sum_all(after(part, grad_low, grad_high))
    input_grad = call(input_grads, shape((count, width), BF), 8, [pad])(hidden_grad, grad_low, grad_high, kernel)
    mixed = call(mix, shape((count, width), BF), 4)(back_outs, slot_cols, hidden)
    in_sum = per_expert(final_in, 3, [out_spec] * 3, in_spec, shape((local, width, held), BF))(own_in, up_in, down_in)
    out_sum = per_expert(final_out, 3, [out_spec] * 3, out_spec, unit_shape)(own_out, up_out, down_out)
    return mixed[None], input_grad[None], in_sum, out_sum, summed[:taps], summed[taps]


def solution(mesh):
    by_block = P("expert", "tm", None)
    by_unit = P("expert", None, "tm")
    return jax.shard_map(
        body,
        mesh=mesh,
        in_specs=(by_block, by_block, by_block, by_unit, by_block, P(), P(), by_block),
        out_specs=(by_block, by_block, by_unit, by_block, P(), P()),
        check_vma=False,
    )
```

```python
import functools

import jax
import jax.numpy as jnp
from jax import lax
from jax.experimental import pallas as pl
from jax.experimental.pallas import tpu as pltpu
from jax.sharding import PartitionSpec as P

BF = jnp.bfloat16
F32 = jnp.float32
EDGE = 16
PARAMS = pltpu.CompilerParams(vmem_limit_bytes=56 * 1024 * 1024)


def ring(count, step):
    return [(i, (i + step) % count) for i in range(count)]


def line(count, step):
    return [(i, i + step) for i in range(count) if 0 <= i + step < count]


def xor(count, step):
    return [(i, i ^ step) for i in range(count)]


def shape(dims, dtype):
    return jax.ShapeDtypeStruct(dims, dtype)


def mm(left, right, dim_left=1, dim_right=0):
    return lax.dot_general(left, right, (((dim_left,), (dim_right,)), ((), ())), preferred_element_type=F32)


def cotangent_slots(experts, capacity, ids_ref, gates_ref, cot_ref, gbuf_ref, rows_ref, cols_ref):
    count = ids_ref.shape[1]
    expert = lax.broadcasted_iota(jnp.int32, (experts, count), 0)
    hot = [(expert == ids_ref[j : j + 1, :]).astype(F32) for j in range(2)]
    frame = lax.broadcasted_iota(jnp.int32, (count, count), 0)
    later = lax.broadcasted_iota(jnp.int32, (count, count), 1)
    earlier = mm((hot[0] + hot[1]).astype(BF), (frame < later).astype(BF))
    rows = [
        ids_ref[j : j + 1, :].astype(F32) * capacity + jnp.sum(hot[j] * earlier, axis=0, keepdims=True)
        for j in range(2)
    ]
    table = jnp.concatenate([gates_ref[...], rows[0], rows[1], jnp.zeros((124, count), F32)], axis=0)
    cols = table.T
    cols_ref[...] = cols
    rows_ref[...] = table[:8]
    place = lax.broadcasted_iota(jnp.int32, (experts * capacity, count), 0)
    spread = [(place == rows[j].astype(jnp.int32)).astype(F32).astype(BF) for j in range(2)]
    cot = cot_ref[...].astype(F32)
    weighted = [(cols[:, j : j + 1] * cot).astype(BF) for j in range(2)]
    gbuf_ref[...] = mm(jnp.concatenate(spread, axis=1), jnp.concatenate(weighted, axis=0)).astype(BF)


def fill(pad, low_ref, mid, high_ref):
    count = mid.shape[0]
    pad[0:EDGE, :] = low_ref[...].astype(F32)
    pad[EDGE : EDGE + count, :] = mid
    pad[EDGE + count : 2 * EDGE + count, :] = high_ref[...].astype(F32)


def convolve(pad, taps_ref, store, count, taps, flip):
    width = pad.shape[1]
    step = 64
    for lane in range(0, width, 128):
        lanes = slice(lane, lane + 128)
        for row in range(0, count, step):
            total = pad[EDGE + row : EDGE + row + step, lanes]
            for k in range(taps):
                at = row + (taps - k if flip else k + 1)
                total = total + taps_ref[k : k + 1, lanes] * pad[at : at + step, lanes]
            store(row, lanes, total)


def norm_slots(capacity_all, frames_ref, low_ref, high_ref, taps_ref, gain_ref, rows_ref, buf_ref, hidden_ref, pad):
    count = frames_ref.shape[0]
    taps = taps_ref.shape[0]
    fill(pad, low_ref, frames_ref[...].astype(F32), high_ref)

    def store(row, lanes, total):
        hidden_ref[row : row + 64, lanes] = total

    convolve(pad, taps_ref, store, count, taps, False)
    hidden = hidden_ref[...]
    inv = lax.rsqrt(jnp.mean(hidden * hidden, axis=-1, keepdims=True) + 1e-06)
    normed = (hidden * inv * gain_ref[...]).astype(BF)
    place = lax.broadcasted_iota(jnp.int32, (capacity_all, count), 0)
    slots = rows_ref[...].astype(jnp.int32)
    spread = ((place == slots[2:3, :]) | (place == slots[3:4, :])).astype(F32).astype(BF)
    buf_ref[...] = mm(spread, normed).astype(BF)


def picks(cols, capacity_all):
    count = cols.shape[0]
    place = lax.broadcasted_iota(jnp.int32, (count, capacity_all), 1)
    slots = cols.astype(jnp.int32)
    return [place == slots[:, 2 + j : 3 + j] for j in range(2)]


def hidden_grads(
    back_ref, cols_ref, hidden_ref, gain_ref, cot_ref, frames_ref, low_ref, high_ref, taps_ref,
    grad_ref, first_ref, last_ref, part_ref, pad,
):
    count = frames_ref.shape[0]
    taps = taps_ref.shape[0]
    width = frames_ref.shape[1]
    fill(pad, low_ref, frames_ref[...].astype(F32), high_ref)
    pick = picks(cols_ref[...], back_ref.shape[0])
    norm_grad = mm((pick[0] | pick[1]).astype(F32).astype(BF), back_ref[...])
    hidden = hidden_ref[...]
    inv = lax.rsqrt(jnp.mean(hidden * hidden, axis=-1, keepdims=True) + 1e-06)
    scaled = norm_grad * gain_ref[...]
    mean = jnp.mean(scaled * hidden, axis=-1, keepdims=True)
    grad_ref[...] = cot_ref[...].astype(F32) + inv * scaled - hidden * (inv * inv * inv * mean)
    first_ref[...] = grad_ref[0:EDGE, :].astype(BF)
    last_ref[...] = grad_ref[count - EDGE : count, :].astype(BF)
    part_ref[taps : taps + 1, :] = jnp.sum(norm_grad * hidden * inv, axis=0, keepdims=True)
    for lane in range(0, width, 128):
        lanes = slice(lane, lane + 128)
        for k in range(taps):
            product = grad_ref[:, lanes] * pad[k + 1 : k + 1 + count, lanes]
            part_ref[k : k + 1, lanes] = jnp.sum(product, axis=0, keepdims=True)


def input_grads(grad_ref, low_ref, high_ref, taps_ref, out_ref, pad):
    count = grad_ref.shape[0]
    fill(pad, low_ref, grad_ref[...], high_ref)

    def store(row, lanes, total):
        out_ref[row : row + 64, lanes] = total.astype(BF)

    convolve(pad, taps_ref, store, count, taps_ref.shape[0], True)


def mix(back_ref, cols_ref, hidden_ref, out_ref):
    cols = cols_ref[...]
    total = hidden_ref[...]
    for j, pick in enumerate(picks(cols, back_ref.shape[0])):
        total = total + cols[:, j : j + 1] * mm(pick.astype(F32).astype(BF), back_ref[...])
    out_ref[...] = total.astype(BF)


def both_rows(own_ref, other_ref):
    width = own_ref.shape[-1]
    return jnp.concatenate([own_ref[...].reshape(-1, width), other_ref[...].reshape(-1, width)], axis=0)


def store_rows(value, own_ref, other_ref):
    half = value.shape[0] // 2
    own_ref[...] = value[:half].astype(BF).reshape(own_ref.shape)
    other_ref[...] = value[half:].astype(BF).reshape(other_ref.shape)


def pack(in_ref, out_ref, packed_ref):
    held, width = out_ref.shape[1:]
    for q in range(width // held):
        rows = slice(q * held, q * held + held)
        packed_ref[0, 0, :, rows] = in_ref[0, rows, :]
    packed_ref[0, 1] = out_ref[0]


def part_in(packed):
    held, width = packed.shape
    return jnp.concatenate([packed[:, q * held : (q + 1) * held] for q in range(width // held)], axis=0)


def far_of(far0, far1, which):
    return jnp.where(pl.program_id(0) == 0, far0[0, which], far1[0, which])


def act_grads(g0, g1, w0, w1, w2, ga_ref):
    grads = both_rows(g0, g1)
    held = w0.shape[2]
    for part, w in enumerate((w0, w1, w2)):
        ga_ref[0, :, part * held : (part + 1) * held] = mm(grads, w[0, 0], 1, 1).astype(BF)


def keep(refs, value):
    for e, ref in enumerate(refs):

        @pl.when(pl.program_id(0) == e)
        def _(ref=ref):
            for which in range(2):
                ref[0, which] = value[which]


def weight_grads(rows, grads, act, pre_grad):
    return mm(pre_grad, rows, 0, 0).astype(BF), mm(act, grads, 0, 0).astype(BF)


def experts_main(
    x0, x1, g0, g1, ga_ref, w0, w1, w2, far0, far1, act_ref, pg_ref, own_ref, other_ref, up_ref, down_ref
):
    rows, grads = both_rows(x0, x1), both_rows(g0, g1)
    held = w0.shape[2]
    parts = [part_in(w[0, 0]) for w in (w0, w1, w2)] + [part_in(far_of(far0, far1, 0))]
    for part in (3, 0, 1, 2):
        columns = slice(part * held, part * held + held)
        pre = mm(rows, parts[part])
        if part == 3:
            act_grad = mm(grads, far_of(far0, far1, 1), 1, 1)
        else:
            act_grad = ga_ref[0, :, columns].astype(F32)
        sig = 0.5 * jnp.tanh(0.5 * pre) + 0.5
        act = (pre * sig).astype(BF)
        pre_grad = (act_grad * (sig * (1.0 + pre * (1.0 - sig)))).astype(BF)
        act_ref[0, :, columns] = act
        pg_ref[0, :, columns] = pre_grad
    expert = pl.program_id(0)
    near = pl.ds(pl.multiple_of((1 + expert) * held, held), held)
    for columns, mine in ((slice(3 * held, 4 * held), 0), (near, 1)):
        pair = weight_grads(rows, grads, act_ref[0, :, columns], pg_ref[0, :, columns])
        for e, ref in ((mine, up_ref), (1 - mine, down_ref)):

            @pl.when(expert == e)
            def _(ref=ref, pair=pair):
                ref[0, 0], ref[0, 1] = pair

    store_rows(mm(pg_ref[0], jnp.concatenate(parts, axis=1), 1, 1), own_ref, other_ref)


def experts_out(act, w0, w1, w2, far0, far1, own_ref, other0, other1):
    parts = [w[0, 0] for w in (w0, w1, w2)] + [far_of(far0, far1, 0)]
    value = mm(act[0], jnp.concatenate(parts, axis=0)).astype(BF)
    half, quarter = value.shape[0] // 2, value.shape[0] // 4
    own_ref[...] = value[:half].reshape(own_ref.shape)
    other0[...] = value[half : half + quarter].reshape(other0.shape)
    other1[...] = value[half + quarter :].reshape(other1.shape)


def add_halves(own, first, second, out):
    for step, ref in enumerate((first, second)):

        @pl.when(pl.program_id(0) == step)
        def _(ref=ref):
            out[...] = (own[...].astype(F32) + ref[...].astype(F32)).astype(BF)


def rest_grads(x0, x1, g0, g1, act0, act1, act2, pg0, pg1, pg2, own_ref, rest_ref):
    rows, grads = both_rows(x0, x1), both_rows(g0, g1)
    first = pl.program_id(0) == 0
    own_ref[0, 0], own_ref[0, 1] = weight_grads(rows, grads, act0[0], pg0[0])
    act, pre_grad = jnp.where(first, act2[0], act1[0]), jnp.where(first, pg2[0], pg1[0])
    rest_ref[0, 0], rest_ref[0, 1] = weight_grads(rows, grads, act, pre_grad)


def final_sum(own, up0, below, above, down1, in_ref, out_ref):
    for e, (first, second) in enumerate(((up0, above), (below, down1))):

        @pl.when(pl.program_id(0) == e)
        def _(first=first, second=second):
            parts = [own[0, w].astype(F32) + first[0, w].astype(F32) + second[0, w].astype(F32) for w in range(2)]
            in_ref[0] = parts[0].T.astype(BF)
            out_ref[0] = parts[1].astype(BF)


def cost(micros):
    return pl.CostEstimate(flops=int(micros * 1e9), transcendentals=0, bytes_accessed=int(micros * 1e6))


def call(kernel, outs, micros, scratch=()):
    return pl.pallas_call(
        kernel, out_shape=outs, scratch_shapes=list(scratch), compiler_params=PARAMS, cost_estimate=cost(micros)
    )


def after(value, *others):
    return lax.optimization_barrier((value,) + others)[0]


def sum_all(part):
    for axis, count, steps in (
        ("expert", 16, (1, 2, 3)),
        ("expert", 16, (4, 8, 12)),
        ("tm", 8, (1,)),
        ("tm", 8, (2, 4, 6)),
    ):
        sent = part.astype(BF)
        for step in steps:
            part = part + lax.ppermute(sent, axis, xor(count, step)).astype(F32)
    return part


def body(frames, routes, gates, w_in, w_out, kernel, gain, cotangent):
    tms = lax.axis_size("tm")
    owners = lax.axis_size("expert")
    count, width = frames.shape[1], frames.shape[2]
    local, held = w_in.shape[0], w_in.shape[2]
    experts = local * owners
    capacity = 4 * count // experts
    slots = experts * capacity
    taps = kernel.shape[0]
    plus, minus, swap = ring(tms, 2), ring(tms, -2), xor(tms, 1)
    block, cot, gain_row = frames[0], cotangent[0], gain[None]
    both = 2 * owners * capacity
    token_shape = shape((owners, local, capacity, width), BF)
    wide_shape = shape((local, both, 4 * held), BF)
    unit_shape = shape((local, held, width), BF)
    one_shape = shape((1, 2, held, width), BF)
    token_spec = pl.BlockSpec((owners, 1, capacity, width), lambda e: (0, e, 0, 0))
    in_spec = pl.BlockSpec((1, width, held), lambda e: (e, 0, 0))
    out_spec = pl.BlockSpec((1, held, width), lambda e: (e, 0, 0))
    packed_spec = pl.BlockSpec((1, 2, held, width), lambda e: (e, 0, 0, 0))
    one_spec = pl.BlockSpec((1, 2, held, width), lambda e: (0, 0, 0, 0))
    wide_spec = pl.BlockSpec((1, both, 4 * held), lambda e: (e, 0, 0))
    most_spec = pl.BlockSpec((1, both, 3 * held), lambda e: (e, 0, 0))

    def part_spec(part):
        return pl.BlockSpec((1, both, held), lambda e: (e, 0, part))

    def per_expert(kernel, micros, in_specs, out_specs, out_shape):
        return pl.pallas_call(
            kernel,
            grid=(local,),
            in_specs=in_specs,
            out_specs=out_specs,
            out_shape=out_shape,
            compiler_params=PARAMS,
            cost_estimate=cost(micros),
        )

    def exchange(rows):
        return lax.all_to_all(
            rows.reshape(owners, local * capacity, width), "expert", split_axis=0, concat_axis=0, tiled=True
        )

    def tokens(value):
        return value.reshape(owners, local, capacity, width)

    low = lax.ppermute(block[count - EDGE :], "tm", line(tms, 1))
    high = lax.ppermute(block[:EDGE], "tm", line(tms, -1))
    packed = per_expert(pack, 3, [in_spec, out_spec], packed_spec, shape((local, 2, held, width), BF))(w_in, w_out)
    packed = after(packed, low, high)
    w_low = lax.ppermute(packed, "tm", plus)
    w_high = lax.ppermute(packed, "tm", minus)

    gbuf, slot_rows, slot_cols = call(
        functools.partial(cotangent_slots, experts, capacity),
        (shape((slots, width), BF), shape((8, count), F32), shape((count, 128), F32)),
        4,
    )(after(routes[0].T, low, high), gates[0].T, cot)
    g_own = exchange(gbuf)
    pad = pltpu.VMEM((count + 2 * EDGE, width), F32)
    buf, hidden = call(
        functools.partial(norm_slots, slots), (shape((slots, width), BF), shape((count, width), F32)), 20, [pad]
    )(block, low, high, kernel, gain_row, slot_rows)
    x_own = exchange(after(buf, g_own))
    g_own = tokens(after(g_own, buf))
    g_other = lax.ppermute(g_own, "tm", swap)
    far0 = lax.ppermute(w_low[:1], "tm", plus)
    far1 = lax.ppermute(w_high[1:], "tm", minus)
    weights = (packed, w_low, w_high, far0, far1)
    weight_specs = [packed_spec] * 3 + [one_spec] * 2
    other_half = pl.BlockSpec((1, 1, held, width), lambda e: (e, 1, 0, 0))
    act_grad = per_expert(
        act_grads, 7, [token_spec] * 2 + [other_half] * 3, most_spec, shape((local, both, 3 * held), BF)
    )(g_own, g_other, packed, w_low, w_high)
    x_own = tokens(after(x_own, act_grad, far0, far1))
    x_other = lax.ppermute(x_own, "tm", swap)
    rows = (x_own, x_other, g_own, g_other)

    half_spec = pl.BlockSpec((1, 1, held, width), lambda e: (e, 0, 0, 0))
    pair_shape = shape((local, 2, held, width), BF)
    act, pre_grad, r_own, r_other, up, down = per_expert(
        experts_main,
        24,
        [token_spec] * 4 + [most_spec] + [half_spec] * 3 + [one_spec] * 2,
        (wide_spec, wide_spec, token_spec, token_spec, packed_spec, packed_spec),
        (wide_shape, wide_shape, token_shape, token_shape, pair_shape, pair_shape),
    )(*rows, act_grad, *weights)
    below = lax.ppermute(up, "tm", plus)
    above = lax.ppermute(down, "tm", minus)

    def summed_cores(own, other):
        swapped = lax.ppermute(other, "tm", swap)
        return (own.astype(F32) + swapped.astype(F32)).astype(BF)

    def back(total):
        return exchange(total).reshape(slots, width)

    far_half = pl.BlockSpec((1, 1, held, width), lambda e: (0, 1, 0, 0))
    r_sum = summed_cores(r_own, r_other)
    back_grads = back(r_sum)
    act, pre_grad = lax.optimization_barrier((act, pre_grad, r_sum))[:2]
    own_grads, rest = per_expert(
        rest_grads,
        0.1,
        [token_spec] * 4 + [part_spec(0), part_spec(1), part_spec(2)] * 2,
        (packed_spec,) * 2,
        (pair_shape,) * 2,
    )(*rows, act, act, act, pre_grad, pre_grad, pre_grad)
    half_tokens = shape((owners // 2, local, capacity, width), BF)
    half_token_spec = pl.BlockSpec((owners // 2, 1, capacity, width), lambda e: (0, e, 0, 0))
    o_own, *o_other = per_expert(
        experts_out,
        0.1,
        [wide_spec] + [other_half] * 3 + [far_half] * 2,
        (token_spec, half_token_spec, half_token_spec),
        (token_shape, half_tokens, half_tokens),
    )(act, *weights)
    o_other = lax.optimization_barrier((*o_other, back_grads, rest))[:2]
    rows_spec = pl.BlockSpec((owners // 2, local, capacity, width), lambda i: (i, 0, 0, 0))
    whole_spec = pl.BlockSpec((owners // 2, local, capacity, width), lambda i: (0, 0, 0, 0))
    o_sum = per_expert(add_halves, 0.1, [rows_spec] + [whole_spec] * 2, rows_spec, token_shape)(
        o_own, *[lax.ppermute(other, "tm", swap) for other in o_other]
    )
    back_grads = after(back_grads, own_grads, rest, o_sum)

    hidden_grad, first, last, part = call(
        hidden_grads,
        (
            shape((count, width), F32),
            shape((EDGE, width), BF),
            shape((EDGE, width), BF),
            shape((taps + 1, width), F32),
        ),
        0.1,
        [pad],
    )(back_grads, slot_cols, hidden, gain_row, cot, block, low, high, kernel)
    grad_low = lax.ppermute(last, "tm", line(tms, 1))
    grad_high = lax.ppermute(first, "tm", line(tms, -1))
    back_outs = back(after(o_sum, back_grads))
    rest = after(rest, first)
    up0 = (rest[:1].astype(F32) + below[:1].astype(F32)).astype(BF)
    down1 = (rest[1:].astype(F32) + above[1:].astype(F32)).astype(BF)
    up0 = lax.ppermute(up0, "tm", plus)
    down1 = lax.ppermute(down1, "tm", minus)
    summed = sum_all(part)
    input_grad = call(input_grads, shape((count, width), BF), 0.1, [pad])(hidden_grad, grad_low, grad_high, kernel)
    mixed = call(mix, shape((count, width), BF), 0.1)(back_outs, slot_cols, hidden)
    second_spec = pl.BlockSpec((1, 2, held, width), lambda e: (1, 0, 0, 0))
    in_sum, out_sum = per_expert(
        final_sum,
        0.1,
        [packed_spec, one_spec, second_spec, one_spec, one_spec],
        (in_spec, out_spec),
        (shape((local, width, held), BF), unit_shape),
    )(own_grads, up0, below, above, down1)
    return mixed[None], input_grad[None], in_sum, out_sum, summed[:taps], summed[taps]


def solution(mesh):
    by_block = P("expert", "tm", None)
    by_unit = P("expert", None, "tm")
    return jax.shard_map(
        body,
        mesh=mesh,
        in_specs=(by_block, by_block, by_block, by_unit, by_block, P(), P(), by_block),
        out_specs=(by_block, by_block, by_unit, by_block, P(), P()),
        check_vma=False,
    )
```

```python
import functools

import jax
import jax.numpy as jnp
from jax import lax
from jax.experimental import pallas as pl
from jax.experimental.pallas import tpu as pltpu
from jax.sharding import PartitionSpec as P

BF = jnp.bfloat16
F32 = jnp.float32
EDGE = 16
PARAMS = pltpu.CompilerParams(vmem_limit_bytes=56 * 1024 * 1024)


def ring(count, step):
    return [(i, (i + step) % count) for i in range(count)]


def line(count, step):
    return [(i, i + step) for i in range(count) if 0 <= i + step < count]


def xor(count, step):
    return [(i, i ^ step) for i in range(count)]


def shape(dims, dtype):
    return jax.ShapeDtypeStruct(dims, dtype)


def mm(left, right, dim_left=1, dim_right=0):
    return lax.dot_general(left, right, (((dim_left,), (dim_right,)), ((), ())), preferred_element_type=F32)


def cotangent_slots(experts, capacity, ids_ref, gates_ref, cot_ref, gbuf_ref, rows_ref, cols_ref):
    count = ids_ref.shape[1]
    expert = lax.broadcasted_iota(jnp.int32, (experts, count), 0)
    hot = [(expert == ids_ref[j : j + 1, :]).astype(F32) for j in range(2)]
    frame = lax.broadcasted_iota(jnp.int32, (count, count), 0)
    later = lax.broadcasted_iota(jnp.int32, (count, count), 1)
    earlier = mm((hot[0] + hot[1]).astype(BF), (frame < later).astype(BF))
    rows = [
        ids_ref[j : j + 1, :].astype(F32) * capacity + jnp.sum(hot[j] * earlier, axis=0, keepdims=True)
        for j in range(2)
    ]
    table = jnp.concatenate([gates_ref[...], rows[0], rows[1], jnp.zeros((124, count), F32)], axis=0)
    cols = table.T
    cols_ref[...] = cols
    rows_ref[...] = table[:8]
    place = lax.broadcasted_iota(jnp.int32, (experts * capacity, count), 0)
    spread = [(place == rows[j].astype(jnp.int32)).astype(F32).astype(BF) for j in range(2)]
    cot = cot_ref[...].astype(F32)
    weighted = [(cols[:, j : j + 1] * cot).astype(BF) for j in range(2)]
    gbuf_ref[...] = mm(jnp.concatenate(spread, axis=1), jnp.concatenate(weighted, axis=0)).astype(BF)


def fill(pad, low_ref, mid, high_ref):
    count = mid.shape[0]
    pad[0:EDGE, :] = low_ref[...].astype(F32)
    pad[EDGE : EDGE + count, :] = mid
    pad[EDGE + count : 2 * EDGE + count, :] = high_ref[...].astype(F32)


def convolve(pad, taps_ref, store, count, taps, flip):
    width = pad.shape[1]
    step = 64
    for lane in range(0, width, 128):
        lanes = slice(lane, lane + 128)
        for row in range(0, count, step):
            total = pad[EDGE + row : EDGE + row + step, lanes]
            for k in range(taps):
                at = row + (taps - k if flip else k + 1)
                total = total + taps_ref[k : k + 1, lanes] * pad[at : at + step, lanes]
            store(row, lanes, total)


def norm_slots(capacity_all, frames_ref, low_ref, high_ref, taps_ref, gain_ref, rows_ref, buf_ref, hidden_ref, pad):
    count = frames_ref.shape[0]
    taps = taps_ref.shape[0]
    fill(pad, low_ref, frames_ref[...].astype(F32), high_ref)

    def store(row, lanes, total):
        hidden_ref[row : row + 64, lanes] = total

    convolve(pad, taps_ref, store, count, taps, False)
    hidden = hidden_ref[...]
    inv = lax.rsqrt(jnp.mean(hidden * hidden, axis=-1, keepdims=True) + 1e-06)
    normed = (hidden * inv * gain_ref[...]).astype(BF)
    place = lax.broadcasted_iota(jnp.int32, (capacity_all, count), 0)
    slots = rows_ref[...].astype(jnp.int32)
    spread = ((place == slots[2:3, :]) | (place == slots[3:4, :])).astype(F32).astype(BF)
    buf_ref[...] = mm(spread, normed).astype(BF)


def picks(cols, capacity_all):
    count = cols.shape[0]
    place = lax.broadcasted_iota(jnp.int32, (count, capacity_all), 1)
    slots = cols.astype(jnp.int32)
    return [place == slots[:, 2 + j : 3 + j] for j in range(2)]


def hidden_grads(
    back_ref, cols_ref, hidden_ref, gain_ref, cot_ref, frames_ref, low_ref, high_ref, taps_ref,
    grad_ref, first_ref, last_ref, part_ref, pad,
):
    count = frames_ref.shape[0]
    taps = taps_ref.shape[0]
    width = frames_ref.shape[1]
    fill(pad, low_ref, frames_ref[...].astype(F32), high_ref)
    pick = picks(cols_ref[...], back_ref.shape[0])
    norm_grad = mm((pick[0] | pick[1]).astype(F32).astype(BF), back_ref[...])
    hidden = hidden_ref[...]
    inv = lax.rsqrt(jnp.mean(hidden * hidden, axis=-1, keepdims=True) + 1e-06)
    scaled = norm_grad * gain_ref[...]
    mean = jnp.mean(scaled * hidden, axis=-1, keepdims=True)
    grad_ref[...] = cot_ref[...].astype(F32) + inv * scaled - hidden * (inv * inv * inv * mean)
    first_ref[...] = grad_ref[0:EDGE, :].astype(BF)
    last_ref[...] = grad_ref[count - EDGE : count, :].astype(BF)
    part_ref[taps : taps + 1, :] = jnp.sum(norm_grad * hidden * inv, axis=0, keepdims=True)
    for lane in range(0, width, 128):
        lanes = slice(lane, lane + 128)
        for k in range(taps):
            product = grad_ref[:, lanes] * pad[k + 1 : k + 1 + count, lanes]
            part_ref[k : k + 1, lanes] = jnp.sum(product, axis=0, keepdims=True)


def input_grads(grad_ref, low_ref, high_ref, taps_ref, out_ref, pad):
    count = grad_ref.shape[0]
    fill(pad, low_ref, grad_ref[...], high_ref)

    def store(row, lanes, total):
        out_ref[row : row + 64, lanes] = total.astype(BF)

    convolve(pad, taps_ref, store, count, taps_ref.shape[0], True)


def mix(back_ref, cols_ref, hidden_ref, out_ref):
    cols = cols_ref[...]
    total = hidden_ref[...]
    for j, pick in enumerate(picks(cols, back_ref.shape[0])):
        total = total + cols[:, j : j + 1] * mm(pick.astype(F32).astype(BF), back_ref[...])
    out_ref[...] = total.astype(BF)


def both_rows(own_ref, other_ref):
    width = own_ref.shape[-1]
    return jnp.concatenate([own_ref[...].reshape(-1, width), other_ref[...].reshape(-1, width)], axis=0)


def store_rows(value, own_ref, other_ref):
    half = value.shape[0] // 2
    own_ref[...] = value[:half].astype(BF).reshape(own_ref.shape)
    other_ref[...] = value[half:].astype(BF).reshape(other_ref.shape)


def pack(in_ref, out_ref, packed_ref):
    held, width = out_ref.shape[1:]
    for q in range(width // held):
        rows = slice(q * held, q * held + held)
        packed_ref[0, 0, :, rows] = in_ref[0, rows, :]
    packed_ref[0, 1] = out_ref[0]


def part_in(packed):
    held, width = packed.shape
    return jnp.concatenate([packed[:, q * held : (q + 1) * held] for q in range(width // held)], axis=0)


def far_of(far0, far1, which):
    return jnp.where(pl.program_id(0) == 0, far0[0, which], far1[0, which])


def act_grads(g0, g1, w0, w1, w2, ga_ref):
    grads = both_rows(g0, g1)
    held = w0.shape[2]
    for part, w in enumerate((w0, w1, w2)):
        ga_ref[0, :, part * held : (part + 1) * held] = mm(grads, w[0, 0], 1, 1).astype(BF)


def keep(refs, value):
    for e, ref in enumerate(refs):

        @pl.when(pl.program_id(0) == e)
        def _(ref=ref):
            for which in range(2):
                ref[0, which] = value[which]


def weight_grads(rows, grads, act, pre_grad):
    return mm(pre_grad, rows, 0, 0).astype(BF), mm(act, grads, 0, 0).astype(BF)


def experts_main(
    x0, x1, g0, g1, ga_ref, w0, w1, w2, far0, far1, act_ref, pg_ref, own_ref, other_ref, up_ref, down_ref
):
    rows, grads = both_rows(x0, x1), both_rows(g0, g1)
    held = w0.shape[2]
    parts = [part_in(w[0, 0]) for w in (w0, w1, w2)] + [part_in(far_of(far0, far1, 0))]
    for part in (3, 0, 1, 2):
        columns = slice(part * held, part * held + held)
        pre = mm(rows, parts[part])
        if part == 3:
            act_grad = mm(grads, far_of(far0, far1, 1), 1, 1)
        else:
            act_grad = ga_ref[0, :, columns].astype(F32)
        sig = 0.5 * jnp.tanh(0.5 * pre) + 0.5
        act = (pre * sig).astype(BF)
        pre_grad = (act_grad * (sig * (1.0 + pre * (1.0 - sig)))).astype(BF)
        act_ref[0, :, columns] = act
        pg_ref[0, :, columns] = pre_grad
    expert = pl.program_id(0)
    near = pl.ds(pl.multiple_of((1 + expert) * held, held), held)
    for columns, mine in ((slice(3 * held, 4 * held), 0), (near, 1)):
        pair = weight_grads(rows, grads, act_ref[0, :, columns], pg_ref[0, :, columns])
        for e, ref in ((mine, up_ref), (1 - mine, down_ref)):

            @pl.when(expert == e)
            def _(ref=ref, pair=pair):
                ref[0, 0], ref[0, 1] = pair

    store_rows(mm(pg_ref[0], jnp.concatenate(parts, axis=1), 1, 1), own_ref, other_ref)


def experts_out(act, w0, w1, w2, far0, far1, own_ref, other0, other1):
    parts = [w[0, 0] for w in (w0, w1, w2)] + [far_of(far0, far1, 0)]
    value = mm(act[0], jnp.concatenate(parts, axis=0)).astype(BF)
    half, quarter = value.shape[0] // 2, value.shape[0] // 4
    own_ref[...] = value[:half].reshape(own_ref.shape)
    other0[...] = value[half : half + quarter].reshape(other0.shape)
    other1[...] = value[half + quarter :].reshape(other1.shape)


def add_halves(own, first, second, out):
    for step, ref in enumerate((first, second)):

        @pl.when(pl.program_id(0) == step)
        def _(ref=ref):
            out[...] = (own[...].astype(F32) + ref[...].astype(F32)).astype(BF)


def rest_grads(x0, x1, g0, g1, act0, act1, act2, pg0, pg1, pg2, own_ref, rest_ref):
    rows, grads = both_rows(x0, x1), both_rows(g0, g1)
    first = pl.program_id(0) == 0
    own_ref[0, 0], own_ref[0, 1] = weight_grads(rows, grads, act0[0], pg0[0])
    act, pre_grad = jnp.where(first, act2[0], act1[0]), jnp.where(first, pg2[0], pg1[0])
    rest_ref[0, 0], rest_ref[0, 1] = weight_grads(rows, grads, act, pre_grad)


def final_sum(own, up0, below, above, down1, in_ref, out_ref):
    for e, (first, second) in enumerate(((up0, above), (below, down1))):

        @pl.when(pl.program_id(0) == e)
        def _(first=first, second=second):
            parts = [own[0, w].astype(F32) + first[0, w].astype(F32) + second[0, w].astype(F32) for w in range(2)]
            in_ref[0] = parts[0].T.astype(BF)
            out_ref[0] = parts[1].astype(BF)


def cost(micros):
    return pl.CostEstimate(flops=int(micros * 1e9), transcendentals=0, bytes_accessed=int(micros * 1e6))


def call(kernel, outs, micros, scratch=()):
    return pl.pallas_call(
        kernel, out_shape=outs, scratch_shapes=list(scratch), compiler_params=PARAMS, cost_estimate=cost(micros)
    )


def after(value, *others):
    return lax.optimization_barrier((value,) + others)[0]


def sum_round(part, axis, count, steps):
    sent = part.astype(BF)
    for step in steps:
        part = part + lax.ppermute(sent, axis, xor(count, step)).astype(F32)
    return part


def body(frames, routes, gates, w_in, w_out, kernel, gain, cotangent):
    tms = lax.axis_size("tm")
    owners = lax.axis_size("expert")
    count, width = frames.shape[1], frames.shape[2]
    local, held = w_in.shape[0], w_in.shape[2]
    experts = local * owners
    capacity = 4 * count // experts
    slots = experts * capacity
    taps = kernel.shape[0]
    plus, minus, swap = ring(tms, 2), ring(tms, -2), xor(tms, 1)
    block, cot, gain_row = frames[0], cotangent[0], gain[None]
    both = 2 * owners * capacity
    token_shape = shape((owners, local, capacity, width), BF)
    wide_shape = shape((local, both, 4 * held), BF)
    unit_shape = shape((local, held, width), BF)
    one_shape = shape((1, 2, held, width), BF)
    token_spec = pl.BlockSpec((owners, 1, capacity, width), lambda e: (0, e, 0, 0))
    in_spec = pl.BlockSpec((1, width, held), lambda e: (e, 0, 0))
    out_spec = pl.BlockSpec((1, held, width), lambda e: (e, 0, 0))
    packed_spec = pl.BlockSpec((1, 2, held, width), lambda e: (e, 0, 0, 0))
    one_spec = pl.BlockSpec((1, 2, held, width), lambda e: (0, 0, 0, 0))
    wide_spec = pl.BlockSpec((1, both, 4 * held), lambda e: (e, 0, 0))
    most_spec = pl.BlockSpec((1, both, 3 * held), lambda e: (e, 0, 0))

    def part_spec(part):
        return pl.BlockSpec((1, both, held), lambda e: (e, 0, part))

    def per_expert(kernel, micros, in_specs, out_specs, out_shape):
        return pl.pallas_call(
            kernel,
            grid=(local,),
            in_specs=in_specs,
            out_specs=out_specs,
            out_shape=out_shape,
            compiler_params=PARAMS,
            cost_estimate=cost(micros),
        )

    def exchange(rows):
        return lax.all_to_all(
            rows.reshape(owners, local * capacity, width), "expert", split_axis=0, concat_axis=0, tiled=True
        )

    def tokens(value):
        return value.reshape(owners, local, capacity, width)

    low = lax.ppermute(block[count - EDGE :], "tm", line(tms, 1))
    high = lax.ppermute(block[:EDGE], "tm", line(tms, -1))
    packed = per_expert(pack, 3, [in_spec, out_spec], packed_spec, shape((local, 2, held, width), BF))(w_in, w_out)
    packed = after(packed, low, high)
    w_low = lax.ppermute(packed, "tm", plus)
    w_high = lax.ppermute(packed, "tm", minus)

    gbuf, slot_rows, slot_cols = call(
        functools.partial(cotangent_slots, experts, capacity),
        (shape((slots, width), BF), shape((8, count), F32), shape((count, 128), F32)),
        4,
    )(after(routes[0].T, low, high), gates[0].T, cot)
    g_own = exchange(gbuf)
    pad = pltpu.VMEM((count + 2 * EDGE, width), F32)
    buf, hidden = call(
        functools.partial(norm_slots, slots), (shape((slots, width), BF), shape((count, width), F32)), 20, [pad]
    )(block, low, high, kernel, gain_row, slot_rows)
    x_own = exchange(after(buf, g_own))
    g_own = tokens(after(g_own, buf))
    g_other = lax.ppermute(g_own, "tm", swap)
    far0 = lax.ppermute(w_low[:1], "tm", plus)
    far1 = lax.ppermute(w_high[1:], "tm", minus)
    weights = (packed, w_low, w_high, far0, far1)
    weight_specs = [packed_spec] * 3 + [one_spec] * 2
    other_half = pl.BlockSpec((1, 1, held, width), lambda e: (e, 1, 0, 0))
    act_grad = per_expert(
        act_grads, 7, [token_spec] * 2 + [other_half] * 3, most_spec, shape((local, both, 3 * held), BF)
    )(g_own, g_other, packed, w_low, w_high)
    x_own = tokens(after(x_own, act_grad, far0, far1))
    x_other = lax.ppermute(x_own, "tm", swap)
    rows = (x_own, x_other, g_own, g_other)

    half_spec = pl.BlockSpec((1, 1, held, width), lambda e: (e, 0, 0, 0))
    pair_shape = shape((local, 2, held, width), BF)
    act, pre_grad, r_own, r_other, up, down = per_expert(
        experts_main,
        24,
        [token_spec] * 4 + [most_spec] + [half_spec] * 3 + [one_spec] * 2,
        (wide_spec, wide_spec, token_spec, token_spec, packed_spec, packed_spec),
        (wide_shape, wide_shape, token_shape, token_shape, pair_shape, pair_shape),
    )(*rows, act_grad, *weights)
    below = lax.ppermute(up, "tm", plus)
    above = lax.ppermute(down, "tm", minus)

    def summed_cores(own, other):
        swapped = lax.ppermute(other, "tm", swap)
        return (own.astype(F32) + swapped.astype(F32)).astype(BF)

    def back(total):
        return exchange(total).reshape(slots, width)

    far_half = pl.BlockSpec((1, 1, held, width), lambda e: (0, 1, 0, 0))
    r_sum = summed_cores(r_own, r_other)
    back_grads = back(r_sum)
    act, pre_grad = lax.optimization_barrier((act, pre_grad, r_sum))[:2]
    own_grads, rest = per_expert(
        rest_grads,
        0.1,
        [token_spec] * 4 + [part_spec(0), part_spec(1), part_spec(2)] * 2,
        (packed_spec,) * 2,
        (pair_shape,) * 2,
    )(*rows, act, act, act, pre_grad, pre_grad, pre_grad)
    half_tokens = shape((owners // 2, local, capacity, width), BF)
    half_token_spec = pl.BlockSpec((owners // 2, 1, capacity, width), lambda e: (0, e, 0, 0))
    o_own, *o_other = per_expert(
        experts_out,
        0.1,
        [wide_spec] + [other_half] * 3 + [far_half] * 2,
        (token_spec, half_token_spec, half_token_spec),
        (token_shape, half_tokens, half_tokens),
    )(act, *weights)
    o_other = lax.optimization_barrier((*o_other, back_grads, rest))[:2]
    rows_spec = pl.BlockSpec((owners // 2, local, capacity, width), lambda i: (i, 0, 0, 0))
    whole_spec = pl.BlockSpec((owners // 2, local, capacity, width), lambda i: (0, 0, 0, 0))
    o_sum = per_expert(add_halves, 0.1, [rows_spec] + [whole_spec] * 2, rows_spec, token_shape)(
        o_own, *[lax.ppermute(other, "tm", swap) for other in o_other]
    )
    back_grads = after(back_grads, own_grads, rest, o_sum)

    hidden_grad, first, last, part = call(
        hidden_grads,
        (
            shape((count, width), F32),
            shape((EDGE, width), BF),
            shape((EDGE, width), BF),
            shape((taps + 1, width), F32),
        ),
        0.1,
        [pad],
    )(back_grads, slot_cols, hidden, gain_row, cot, block, low, high, kernel)
    grad_low = lax.ppermute(last, "tm", line(tms, 1))
    grad_high = lax.ppermute(first, "tm", line(tms, -1))
    back_outs = back(after(o_sum, back_grads))
    rest = after(rest, first)
    up0 = (rest[:1].astype(F32) + below[:1].astype(F32)).astype(BF)
    down1 = (rest[1:].astype(F32) + above[1:].astype(F32)).astype(BF)
    part, up0, down1 = lax.optimization_barrier((part, up0, down1))
    part = sum_round(part, "tm", tms, (1,))
    part = sum_round(part, "tm", tms, (2, 4, 6))
    up0, down1 = lax.optimization_barrier((up0, down1, part, grad_low, grad_high))[:2]
    up0 = lax.ppermute(up0, "tm", plus)
    down1 = lax.ppermute(down1, "tm", minus)
    input_grad = call(input_grads, shape((count, width), BF), 0.1, [pad])(hidden_grad, grad_low, grad_high, kernel)
    part = sum_round(after(part, input_grad), "expert", owners, (1, 2, 3))
    mixed = call(mix, shape((count, width), BF), 0.1)(back_outs, slot_cols, hidden)
    summed = sum_round(after(part, mixed), "expert", owners, (4, 8, 12))
    second_spec = pl.BlockSpec((1, 2, held, width), lambda e: (1, 0, 0, 0))
    in_sum, out_sum = per_expert(
        final_sum,
        0.1,
        [packed_spec, one_spec, second_spec, one_spec, one_spec],
        (in_spec, out_spec),
        (shape((local, width, held), BF), unit_shape),
    )(own_grads, up0, below, above, down1)
    return mixed[None], input_grad[None], in_sum, out_sum, summed[:taps], summed[taps]


def solution(mesh):
    by_block = P("expert", "tm", None)
    by_unit = P("expert", None, "tm")
    return jax.shard_map(
        body,
        mesh=mesh,
        in_specs=(by_block, by_block, by_block, by_unit, by_block, P(), P(), by_block),
        out_specs=(by_block, by_block, by_unit, by_block, P(), P()),
        check_vma=False,
    )
```

```python
import functools

import jax
import jax.numpy as jnp
from jax import lax
from jax.experimental import pallas as pl
from jax.experimental.pallas import tpu as pltpu
from jax.sharding import PartitionSpec as P

BF = jnp.bfloat16
F32 = jnp.float32
EDGE = 16
PARAMS = pltpu.CompilerParams(vmem_limit_bytes=56 * 1024 * 1024)


def ring(count, step):
    return [(i, (i + step) % count) for i in range(count)]


def line(count, step):
    return [(i, i + step) for i in range(count) if 0 <= i + step < count]


def xor(count, step):
    return [(i, i ^ step) for i in range(count)]


def shape(dims, dtype):
    return jax.ShapeDtypeStruct(dims, dtype)


def mm(left, right, dim_left=1, dim_right=0):
    return lax.dot_general(left, right, (((dim_left,), (dim_right,)), ((), ())), preferred_element_type=F32)


def cotangent_slots(experts, capacity, ids_ref, gates_ref, cot_ref, gbuf_ref, rows_ref, cols_ref):
    count = ids_ref.shape[1]
    expert = lax.broadcasted_iota(jnp.int32, (experts, count), 0)
    hot = [(expert == ids_ref[j : j + 1, :]).astype(F32) for j in range(2)]
    frame = lax.broadcasted_iota(jnp.int32, (count, count), 0)
    later = lax.broadcasted_iota(jnp.int32, (count, count), 1)
    earlier = mm((hot[0] + hot[1]).astype(BF), (frame < later).astype(BF))
    rows = [
        ids_ref[j : j + 1, :].astype(F32) * capacity + jnp.sum(hot[j] * earlier, axis=0, keepdims=True)
        for j in range(2)
    ]
    table = jnp.concatenate([gates_ref[...], rows[0], rows[1], jnp.zeros((124, count), F32)], axis=0)
    cols = table.T
    cols_ref[...] = cols
    rows_ref[...] = table[:8]
    place = lax.broadcasted_iota(jnp.int32, (experts * capacity, count), 0)
    spread = [(place == rows[j].astype(jnp.int32)).astype(F32).astype(BF) for j in range(2)]
    cot = cot_ref[...].astype(F32)
    weighted = [(cols[:, j : j + 1] * cot).astype(BF) for j in range(2)]
    gbuf_ref[...] = mm(jnp.concatenate(spread, axis=1), jnp.concatenate(weighted, axis=0)).astype(BF)


def fill(pad, low_ref, mid, high_ref):
    count = mid.shape[0]
    pad[0:EDGE, :] = low_ref[...].astype(F32)
    pad[EDGE : EDGE + count, :] = mid
    pad[EDGE + count : 2 * EDGE + count, :] = high_ref[...].astype(F32)


def convolve(pad, taps_ref, store, count, taps, flip):
    width = pad.shape[1]
    step = 64
    for lane in range(0, width, 128):
        lanes = slice(lane, lane + 128)
        for row in range(0, count, step):
            total = pad[EDGE + row : EDGE + row + step, lanes]
            for k in range(taps):
                at = row + (taps - k if flip else k + 1)
                total = total + taps_ref[k : k + 1, lanes] * pad[at : at + step, lanes]
            store(row, lanes, total)


def norm_slots(capacity_all, frames_ref, low_ref, high_ref, taps_ref, gain_ref, rows_ref, buf_ref, hidden_ref, pad):
    count = frames_ref.shape[0]
    taps = taps_ref.shape[0]
    fill(pad, low_ref, frames_ref[...].astype(F32), high_ref)

    def store(row, lanes, total):
        hidden_ref[row : row + 64, lanes] = total

    convolve(pad, taps_ref, store, count, taps, False)
    hidden = hidden_ref[...]
    inv = lax.rsqrt(jnp.mean(hidden * hidden, axis=-1, keepdims=True) + 1e-06)
    normed = (hidden * inv * gain_ref[...]).astype(BF)
    place = lax.broadcasted_iota(jnp.int32, (capacity_all, count), 0)
    slots = rows_ref[...].astype(jnp.int32)
    spread = ((place == slots[2:3, :]) | (place == slots[3:4, :])).astype(F32).astype(BF)
    buf_ref[...] = mm(spread, normed).astype(BF)


def picks(cols, capacity_all):
    count = cols.shape[0]
    place = lax.broadcasted_iota(jnp.int32, (count, capacity_all), 1)
    slots = cols.astype(jnp.int32)
    return [place == slots[:, 2 + j : 3 + j] for j in range(2)]


def hidden_grads(
    back_ref, cols_ref, hidden_ref, gain_ref, cot_ref, frames_ref, low_ref, high_ref, taps_ref,
    grad_ref, first_ref, last_ref, part_ref, pad,
):
    count = frames_ref.shape[0]
    taps = taps_ref.shape[0]
    width = frames_ref.shape[1]
    fill(pad, low_ref, frames_ref[...].astype(F32), high_ref)
    pick = picks(cols_ref[...], back_ref.shape[0])
    norm_grad = mm((pick[0] | pick[1]).astype(F32).astype(BF), back_ref[...])
    hidden = hidden_ref[...]
    inv = lax.rsqrt(jnp.mean(hidden * hidden, axis=-1, keepdims=True) + 1e-06)
    scaled = norm_grad * gain_ref[...]
    mean = jnp.mean(scaled * hidden, axis=-1, keepdims=True)
    grad_ref[...] = cot_ref[...].astype(F32) + inv * scaled - hidden * (inv * inv * inv * mean)
    first_ref[...] = grad_ref[0:EDGE, :].astype(BF)
    last_ref[...] = grad_ref[count - EDGE : count, :].astype(BF)
    part_ref[taps : taps + 1, :] = jnp.sum(norm_grad * hidden * inv, axis=0, keepdims=True)
    for lane in range(0, width, 128):
        lanes = slice(lane, lane + 128)
        for k in range(taps):
            product = grad_ref[:, lanes] * pad[k + 1 : k + 1 + count, lanes]
            part_ref[k : k + 1, lanes] = jnp.sum(product, axis=0, keepdims=True)


def input_grads(grad_ref, low_ref, high_ref, taps_ref, out_ref, pad):
    count = grad_ref.shape[0]
    fill(pad, low_ref, grad_ref[...], high_ref)

    def store(row, lanes, total):
        out_ref[row : row + 64, lanes] = total.astype(BF)

    convolve(pad, taps_ref, store, count, taps_ref.shape[0], True)


def mix(back_ref, cols_ref, hidden_ref, out_ref):
    cols = cols_ref[...]
    total = hidden_ref[...]
    for j, pick in enumerate(picks(cols, back_ref.shape[0])):
        total = total + cols[:, j : j + 1] * mm(pick.astype(F32).astype(BF), back_ref[...])
    out_ref[...] = total.astype(BF)


def both_rows(own_ref, other_ref):
    width = own_ref.shape[-1]
    return jnp.concatenate([own_ref[...].reshape(-1, width), other_ref[...].reshape(-1, width)], axis=0)


def store_rows(value, own_ref, other_ref):
    half = value.shape[0] // 2
    own_ref[...] = value[:half].astype(BF).reshape(own_ref.shape)
    other_ref[...] = value[half:].astype(BF).reshape(other_ref.shape)


def pack(in_ref, out_ref, packed_ref):
    held, width = out_ref.shape[1:]
    for q in range(width // held):
        rows = slice(q * held, q * held + held)
        packed_ref[0, 0, :, rows] = in_ref[0, rows, :]
    packed_ref[0, 1] = out_ref[0]


def part_in(packed):
    held, width = packed.shape
    return jnp.concatenate([packed[:, q * held : (q + 1) * held] for q in range(width // held)], axis=0)


def far_of(far0, far1, which):
    return jnp.where(pl.program_id(0) == 0, far0[0, which], far1[0, which])


def act_grads(g0, g1, w0, w1, w2, ga_ref):
    grads = both_rows(g0, g1)
    held = w0.shape[2]
    for part, w in enumerate((w0, w1, w2)):
        ga_ref[0, :, part * held : (part + 1) * held] = mm(grads, w[0, 0], 1, 1).astype(BF)


def keep(refs, value):
    for e, ref in enumerate(refs):

        @pl.when(pl.program_id(0) == e)
        def _(ref=ref):
            for which in range(2):
                ref[0, which] = value[which]


def weight_grads(rows, grads, act, pre_grad):
    return mm(pre_grad, rows, 0, 0).astype(BF), mm(act, grads, 0, 0).astype(BF)


def experts_main(
    x0, x1, g0, g1, ga_ref, w0, w1, w2, far0, far1, act_ref, pg_ref, own_ref, other_ref, up_ref, down_ref
):
    rows, grads = both_rows(x0, x1), both_rows(g0, g1)
    held = w0.shape[2]
    parts = [part_in(w[0, 0]) for w in (w0, w1, w2)] + [part_in(far_of(far0, far1, 0))]
    for part in (3, 0, 1, 2):
        columns = slice(part * held, part * held + held)
        pre = mm(rows, parts[part])
        if part == 3:
            act_grad = mm(grads, far_of(far0, far1, 1), 1, 1)
        else:
            act_grad = ga_ref[0, :, columns].astype(F32)
        sig = 0.5 * jnp.tanh(0.5 * pre) + 0.5
        act = (pre * sig).astype(BF)
        pre_grad = (act_grad * (sig * (1.0 + pre * (1.0 - sig)))).astype(BF)
        act_ref[0, :, columns] = act
        pg_ref[0, :, columns] = pre_grad
    expert = pl.program_id(0)
    near = pl.ds(pl.multiple_of((1 + expert) * held, held), held)
    for columns, mine in ((slice(3 * held, 4 * held), 0), (near, 1)):
        pair = weight_grads(rows, grads, act_ref[0, :, columns], pg_ref[0, :, columns])
        for e, ref in ((mine, up_ref), (1 - mine, down_ref)):

            @pl.when(expert == e)
            def _(ref=ref, pair=pair):
                ref[0, 0], ref[0, 1] = pair

    store_rows(mm(pg_ref[0], jnp.concatenate(parts, axis=1), 1, 1), own_ref, other_ref)


def experts_out(act, w0, w1, w2, far0, far1, own_ref, other0, other1):
    parts = [w[0, 0] for w in (w0, w1, w2)] + [far_of(far0, far1, 0)]
    value = mm(act[0], jnp.concatenate(parts, axis=0)).astype(BF)
    half, quarter = value.shape[0] // 2, value.shape[0] // 4
    own_ref[...] = value[:half].reshape(own_ref.shape)
    other0[...] = value[half : half + quarter].reshape(other0.shape)
    other1[...] = value[half + quarter :].reshape(other1.shape)


def add_halves(own, first, second, out):
    for step, ref in enumerate((first, second)):

        @pl.when(pl.program_id(0) == step)
        def _(ref=ref):
            out[...] = (own[...].astype(F32) + ref[...].astype(F32)).astype(BF)


def rest_grads(x0, x1, g0, g1, act0, act1, act2, pg0, pg1, pg2, own_ref, rest_ref):
    rows, grads = both_rows(x0, x1), both_rows(g0, g1)
    first = pl.program_id(0) == 0
    own_ref[0, 0], own_ref[0, 1] = weight_grads(rows, grads, act0[0], pg0[0])
    act, pre_grad = jnp.where(first, act2[0], act1[0]), jnp.where(first, pg2[0], pg1[0])
    rest_ref[0, 0], rest_ref[0, 1] = weight_grads(rows, grads, act, pre_grad)


def final_sum(own, up0, below, above, down1, in_ref, out_ref):
    for e, (first, second) in enumerate(((up0, above), (below, down1))):

        @pl.when(pl.program_id(0) == e)
        def _(first=first, second=second):
            parts = [own[0, w].astype(F32) + first[0, w].astype(F32) + second[0, w].astype(F32) for w in range(2)]
            in_ref[0] = parts[0].T.astype(BF)
            out_ref[0] = parts[1].astype(BF)


def cost(micros):
    return pl.CostEstimate(flops=int(micros * 1e9), transcendentals=0, bytes_accessed=int(micros * 1e6))


def call(kernel, outs, micros, scratch=()):
    return pl.pallas_call(
        kernel, out_shape=outs, scratch_shapes=list(scratch), compiler_params=PARAMS, cost_estimate=cost(micros)
    )


def after(value, *others):
    return lax.optimization_barrier((value,) + others)[0]


def sum_round(part, axis, count, steps):
    sent = part.astype(BF)
    for step in steps:
        part = part + lax.ppermute(sent, axis, xor(count, step)).astype(F32)
    return part


def body(frames, routes, gates, w_in, w_out, kernel, gain, cotangent):
    tms = lax.axis_size("tm")
    owners = lax.axis_size("expert")
    count, width = frames.shape[1], frames.shape[2]
    local, held = w_in.shape[0], w_in.shape[2]
    experts = local * owners
    capacity = 4 * count // experts
    slots = experts * capacity
    taps = kernel.shape[0]
    plus, minus, swap = ring(tms, 2), ring(tms, -2), xor(tms, 1)
    block, cot, gain_row = frames[0], cotangent[0], gain[None]
    both = 2 * owners * capacity
    token_shape = shape((owners, local, capacity, width), BF)
    wide_shape = shape((local, both, 4 * held), BF)
    unit_shape = shape((local, held, width), BF)
    one_shape = shape((1, 2, held, width), BF)
    token_spec = pl.BlockSpec((owners, 1, capacity, width), lambda e: (0, e, 0, 0))
    in_spec = pl.BlockSpec((1, width, held), lambda e: (e, 0, 0))
    out_spec = pl.BlockSpec((1, held, width), lambda e: (e, 0, 0))
    packed_spec = pl.BlockSpec((1, 2, held, width), lambda e: (e, 0, 0, 0))
    one_spec = pl.BlockSpec((1, 2, held, width), lambda e: (0, 0, 0, 0))
    wide_spec = pl.BlockSpec((1, both, 4 * held), lambda e: (e, 0, 0))
    most_spec = pl.BlockSpec((1, both, 3 * held), lambda e: (e, 0, 0))

    def part_spec(part):
        return pl.BlockSpec((1, both, held), lambda e: (e, 0, part))

    def per_expert(kernel, micros, in_specs, out_specs, out_shape):
        return pl.pallas_call(
            kernel,
            grid=(local,),
            in_specs=in_specs,
            out_specs=out_specs,
            out_shape=out_shape,
            compiler_params=PARAMS,
            cost_estimate=cost(micros),
        )

    def exchange(rows):
        return lax.all_to_all(
            rows.reshape(owners, local * capacity, width), "expert", split_axis=0, concat_axis=0, tiled=True
        )

    def tokens(value):
        return value.reshape(owners, local, capacity, width)

    low = lax.ppermute(block[count - EDGE :], "tm", line(tms, 1))
    high = lax.ppermute(block[:EDGE], "tm", line(tms, -1))
    packed = per_expert(pack, 3, [in_spec, out_spec], packed_spec, shape((local, 2, held, width), BF))(w_in, w_out)
    packed = after(packed, low, high)
    w_low = lax.ppermute(packed, "tm", plus)
    w_high = lax.ppermute(packed, "tm", minus)

    gbuf, slot_rows, slot_cols = call(
        functools.partial(cotangent_slots, experts, capacity),
        (shape((slots, width), BF), shape((8, count), F32), shape((count, 128), F32)),
        4,
    )(after(routes[0].T, low, high), gates[0].T, cot)
    g_own = exchange(gbuf)
    pad = pltpu.VMEM((count + 2 * EDGE, width), F32)
    buf, hidden = call(
        functools.partial(norm_slots, slots), (shape((slots, width), BF), shape((count, width), F32)), 20, [pad]
    )(block, low, high, kernel, gain_row, slot_rows)
    x_own = exchange(after(buf, g_own))
    g_own = tokens(after(g_own, buf))
    g_other = lax.ppermute(g_own, "tm", swap)
    far0 = lax.ppermute(w_low[:1], "tm", plus)
    far1 = lax.ppermute(w_high[1:], "tm", minus)
    weights = (packed, w_low, w_high, far0, far1)
    weight_specs = [packed_spec] * 3 + [one_spec] * 2
    other_half = pl.BlockSpec((1, 1, held, width), lambda e: (e, 1, 0, 0))
    act_grad = per_expert(
        act_grads, 7, [token_spec] * 2 + [other_half] * 3, most_spec, shape((local, both, 3 * held), BF)
    )(g_own, g_other, packed, w_low, w_high)
    x_own = tokens(after(x_own, act_grad, far0, far1))
    x_other = lax.ppermute(x_own, "tm", swap)
    rows = (x_own, x_other, g_own, g_other)

    half_spec = pl.BlockSpec((1, 1, held, width), lambda e: (e, 0, 0, 0))
    pair_shape = shape((local, 2, held, width), BF)
    act, pre_grad, r_own, r_other, up, down = per_expert(
        experts_main,
        24,
        [token_spec] * 4 + [most_spec] + [half_spec] * 3 + [one_spec] * 2,
        (wide_spec, wide_spec, token_spec, token_spec, packed_spec, packed_spec),
        (wide_shape, wide_shape, token_shape, token_shape, pair_shape, pair_shape),
    )(*rows, act_grad, *weights)
    below = lax.ppermute(up, "tm", plus)
    above = lax.ppermute(down, "tm", minus)

    def summed_cores(own, other):
        swapped = lax.ppermute(other, "tm", swap)
        return (own.astype(F32) + swapped.astype(F32)).astype(BF)

    def back(total):
        return exchange(total).reshape(slots, width)

    far_half = pl.BlockSpec((1, 1, held, width), lambda e: (0, 1, 0, 0))
    r_sum = summed_cores(r_own, r_other)
    back_grads = back(r_sum)
    act, pre_grad = lax.optimization_barrier((act, pre_grad, r_sum))[:2]
    own_grads, rest = per_expert(
        rest_grads,
        0.1,
        [token_spec] * 4 + [part_spec(0), part_spec(1), part_spec(2)] * 2,
        (packed_spec,) * 2,
        (pair_shape,) * 2,
    )(*rows, act, act, act, pre_grad, pre_grad, pre_grad)
    half_tokens = shape((owners // 2, local, capacity, width), BF)
    half_token_spec = pl.BlockSpec((owners // 2, 1, capacity, width), lambda e: (0, e, 0, 0))
    o_own, *o_other = per_expert(
        experts_out,
        0.1,
        [wide_spec] + [other_half] * 3 + [far_half] * 2,
        (token_spec, half_token_spec, half_token_spec),
        (token_shape, half_tokens, half_tokens),
    )(act, *weights)
    o_other = lax.optimization_barrier((*o_other, back_grads, rest))[:2]
    rows_spec = pl.BlockSpec((owners // 2, local, capacity, width), lambda i: (i, 0, 0, 0))
    whole_spec = pl.BlockSpec((owners // 2, local, capacity, width), lambda i: (0, 0, 0, 0))
    o_sum = per_expert(add_halves, 0.1, [rows_spec] + [whole_spec] * 2, rows_spec, token_shape)(
        o_own, *[lax.ppermute(other, "tm", swap) for other in o_other]
    )
    back_grads = after(back_grads, own_grads, rest, o_sum)

    hidden_grad, first, last, part = call(
        hidden_grads,
        (
            shape((count, width), F32),
            shape((EDGE, width), BF),
            shape((EDGE, width), BF),
            shape((taps + 1, width), F32),
        ),
        0.1,
        [pad],
    )(back_grads, slot_cols, hidden, gain_row, cot, block, low, high, kernel)
    grad_low = lax.ppermute(last, "tm", line(tms, 1))
    grad_high = lax.ppermute(first, "tm", line(tms, -1))
    back_outs = back(after(o_sum, back_grads))
    rest = after(rest, first)
    up0 = (rest[:1].astype(F32) + below[:1].astype(F32)).astype(BF)
    down1 = (rest[1:].astype(F32) + above[1:].astype(F32)).astype(BF)
    part, up0, down1 = lax.optimization_barrier((part, up0, down1))
    part = sum_round(part, "tm", tms, (1,))
    part = sum_round(part, "tm", tms, (2, 4, 6))
    up0, down1 = lax.optimization_barrier((up0, down1, part, grad_low, grad_high))[:2]
    up0 = lax.ppermute(up0, "tm", plus)
    down1 = lax.ppermute(down1, "tm", minus)
    input_grad = call(input_grads, shape((count, width), BF), 0.1, [pad])(hidden_grad, grad_low, grad_high, kernel)
    part = sum_round(part, "expert", owners, (1, 2, 3))
    mixed = call(mix, shape((count, width), BF), 0.1)(back_outs, slot_cols, hidden)
    summed = sum_round(after(part, input_grad, mixed), "expert", owners, (4, 8, 12))
    second_spec = pl.BlockSpec((1, 2, held, width), lambda e: (1, 0, 0, 0))
    in_sum, out_sum = per_expert(
        final_sum,
        0.1,
        [packed_spec, one_spec, second_spec, one_spec, one_spec],
        (in_spec, out_spec),
        (shape((local, width, held), BF), unit_shape),
    )(own_grads, up0, below, above, down1)
    return mixed[None], input_grad[None], in_sum, out_sum, summed[:taps], summed[taps]


def solution(mesh):
    by_block = P("expert", "tm", None)
    by_unit = P("expert", None, "tm")
    return jax.shard_map(
        body,
        mesh=mesh,
        in_specs=(by_block, by_block, by_block, by_unit, by_block, P(), P(), by_block),
        out_specs=(by_block, by_block, by_unit, by_block, P(), P()),
        check_vma=False,
    )
```
